128 devices in a mesh: req: 4 (over y), blk: 32 (over z, x, core).
Axes of the slice: x: 4, y: 4, z: 4, core: 2. Of those that a mesh axis runs over, the one named last changes fastest.
Arguments:
- queries: bfloat16 [4, 4096, 4096], P('req', 'blk'), may hold values from -12.5 to 12.5
- fresh_cache: bfloat16 [4, 4096, 1024], P('req', 'blk'), may hold values from -12.5 to 12.5
- page_store: bfloat16 [512, 32, 1024], P(('req', 'blk')), may hold values from -12.5 to 12.5
- page_table: int32 [4, 128], replicated, may hold values from 0 to 511, as said below
- prefix_lengths: int32 [4], replicated, may hold values from 819 to 4096, as said below
Outputs:
- attended: bfloat16 [4, 4096, 4096], P('req', 'blk')
- new_pages: bfloat16 [4, 4, 32, 32, 1024], P('req', None, 'blk')
The draws below stay inside these ranges and needn't reach their ends.
Inputs may be any that keep to these rules, and one draw needn't show every extreme that they name: page_table[r, p] is the slot of page_store holding prefix page p of request r; all slots are distinct and cover the store; slot s holds a page of request (s % 4), so each block of 4 slots holds exactly one page of every request. `prefix_lengths`: some request has a prefix of exactly 4096 tokens.
All inputs are finite; a program needn't handle non-finite values.
Results may differ from the reference program's by a relative error of at most 0.0065.
Values may be sent and summed in bfloat16 or wider, within the bound.
A program may use at most 192 MiB of HBM per device.

```python
import math
import jax
import jax.numpy as jnp
from jax import lax

H = 32
KVH = 4
HD = 128
PAGES_DEV_REQ = 1
PAGE = 32
REQS = 4
SUFFIX = 4096
PREFIX_PAGES = 128
PREFIX_MAX = 4096
SLOTS = 512
N_REQ = 4
N_BLK = 32


def draw_queries(key, part):
    key = jax.random.fold_in(key, 1)
    drawn = 2.0 * jax.random.normal(key, (REQS, SUFFIX, H, HD), jnp.float32)
    return jnp.clip(drawn, -12.5, 12.5).reshape(REQS, SUFFIX, H * HD).astype(jnp.bfloat16)


def draw_fresh_cache(key, part):
    key = jax.random.fold_in(key, 2)
    key_part, value_part = jax.random.split(key, 2)
    keys_drawn = jax.random.normal(key_part, (REQS, SUFFIX, KVH, HD), jnp.float32)
    values_drawn = 3.0 * jax.random.normal(value_part, (REQS, SUFFIX, KVH, HD), jnp.float32)
    joined = jnp.stack([keys_drawn, values_drawn], axis=2)
    return jnp.clip(joined, -12.5, 12.5).reshape(REQS, SUFFIX, 2 * KVH * HD).astype(jnp.bfloat16)


def draw_page_store(key, part):
    key = jax.random.fold_in(key, 3)
    key_part, value_part = jax.random.split(key, 2)
    keys_drawn = jax.random.normal(key_part, (SLOTS, PAGE, KVH, HD), jnp.float32)
    values_drawn = 3.0 * jax.random.normal(value_part, (SLOTS, PAGE, KVH, HD), jnp.float32)
    joined = jnp.stack([keys_drawn, values_drawn], axis=2)
    return jnp.clip(joined, -12.5, 12.5).reshape(SLOTS, PAGE, 2 * KVH * HD).astype(jnp.bfloat16)


def draw_page_table(key, part):
    key = jax.random.fold_in(key, 5)
    request_keys = jax.random.split(key, REQS)
    placed = jax.vmap(lambda one_key: jax.random.permutation(one_key, PREFIX_PAGES))(request_keys)
    owner = placed // PAGES_DEV_REQ
    within = placed % PAGES_DEV_REQ
    request = jnp.arange(REQS, dtype=jnp.int32)[:, None]
    return (owner * (REQS * PAGES_DEV_REQ) + request * PAGES_DEV_REQ + within).astype(jnp.int32)


def draw_prefix_lengths(key, part):
    key = jax.random.fold_in(key, 6)
    first_key, second_key = jax.random.split(key)
    drawn = jax.random.randint(first_key, (REQS,), PREFIX_MAX // 5, PREFIX_MAX + 1)
    longest = jax.random.randint(second_key, (), 0, REQS)
    return jnp.where(jnp.arange(REQS) == longest, PREFIX_MAX, drawn).astype(jnp.int32)


def setup_inputs(seed: int = 0) -> dict:
    streams_of = jax.random.split(jax.random.key(seed), 6)
    queries = draw_queries(jax.random.fold_in(streams_of[5], 71), 0)
    fresh_cache = draw_fresh_cache(jax.random.fold_in(streams_of[5], 71), 0)
    page_store = draw_page_store(jax.random.fold_in(streams_of[5], 71), 0)
    page_table = draw_page_table(jax.random.fold_in(streams_of[5], 71), 0)
    prefix_lengths = draw_prefix_lengths(jax.random.fold_in(streams_of[5], 71), 0)
    return dict(queries=queries, fresh_cache=fresh_cache, page_store=page_store, page_table=page_table, prefix_lengths=prefix_lengths)


NEG_FILL = -1e+30

def head_attend(query_rows, key_rows, value_rows, allowed):
    scores = jnp.einsum('bjd,kd->jbk', query_rows, key_rows) * (1.0 / math.sqrt(HD))
    scores = jnp.where(allowed[None], scores, NEG_FILL)
    row_max = lax.optimization_barrier(jnp.max(scores, axis=-1, keepdims=True))
    weights = jnp.where(allowed[None], jnp.exp(scores - row_max), 0.0)
    totals = lax.optimization_barrier(jnp.sum(weights, axis=-1))
    rounded = lax.optimization_barrier(weights.astype(jnp.bfloat16)).astype(jnp.float32)
    mixture = jnp.einsum('jbk,kd->bjd', rounded, value_rows)
    return mixture / jnp.transpose(totals)[:, :, None]

def reference(queries, fresh_cache, page_store, page_table, prefix_lengths):
    group_size = H // KVH
    block_rows = min(512, SUFFIX)
    block_count = SUFFIX // block_rows
    key_index = jnp.arange(PREFIX_MAX + SUFFIX, dtype=jnp.int32)

    def one_request(operands):
        query_req, fresh_req, table_row, length = operands
        paged_rows = page_store[table_row].reshape(PREFIX_MAX, 2, KVH, HD)
        fresh_rows = fresh_req.reshape(SUFFIX, 2, KVH, HD)
        joined = jnp.concatenate([paged_rows, fresh_rows], axis=0).astype(jnp.float32)
        key_heads = jnp.transpose(joined[:, 0], (1, 0, 2))
        value_heads = jnp.transpose(joined[:, 1], (1, 0, 2))
        query_blocks = query_req.reshape(block_count, block_rows, KVH, group_size, HD)

        def one_block(block_operands):
            query_block, first_row = block_operands
            query_pos = first_row + jnp.arange(block_rows, dtype=jnp.int32)
            prefix_ok = (key_index < PREFIX_MAX) & (key_index < length)
            suffix_ok = (key_index >= PREFIX_MAX) & (key_index - PREFIX_MAX <= query_pos[:, None])
            allowed = prefix_ok[None, :] | suffix_ok
            per_head = lax.map(lambda head_operands: head_attend(head_operands[0], head_operands[1], head_operands[2], allowed), (jnp.transpose(query_block.astype(jnp.float32), (1, 0, 2, 3)), key_heads, value_heads))
            return jnp.transpose(per_head, (1, 0, 2, 3)).reshape(block_rows, H * HD).astype(jnp.bfloat16)
        starts = jnp.arange(block_count, dtype=jnp.int32) * block_rows
        return lax.map(one_block, (query_blocks, starts)).reshape(SUFFIX, H * HD)
    attended = lax.map(one_request, (queries, fresh_cache, page_table, prefix_lengths))
    new_pages = jnp.transpose(fresh_cache.reshape(REQS, N_BLK, N_REQ, PAGE, 2 * KVH * HD), (2, 0, 1, 3, 4))
    return (attended, new_pages)
```

```python
import functools
import math

import jax
import jax.numpy as jnp
from jax import lax
from jax.experimental import pallas as pl
from jax.experimental.pallas import tpu as pltpu
from jax.sharding import PartitionSpec as P

H = 32
KVH = 4
HD = 128
GROUP = H // KVH
TOK = 128
PAGE = 32
CHUNK = 1024
ROWS = GROUP * TOK
NEG = -1e30
SCALE = math.log2(math.e) / math.sqrt(HD)
MESH = pl.DeviceIdType.MESH
BLOCK = 256


def kernel(
    queries, fresh, pages, table, lengths, attended, written,
    kvx, raw, q_raw, q_two, acc, top, o_buf, limits,
    pg_send, pg_recv, fr_send, fr_recv, q_send, q_recv, o_send, o_recv,
    np_send, np_recv, pre_send, pre_recv, suf_send, suf_recv,
):
    y = lax.axis_index("req")
    blk = lax.axis_index("blk")
    z, x, c = blk // 8, (blk // 2) % 4, blk % 2

    def at(dy, dz, dx, dc):
        z2, x2 = lax.rem(z + dz, 4), lax.rem(x + dx, 4)
        c2 = 1 - c if dc else c
        return (lax.rem(y + dy, 4), z2 * 8 + x2 * 2 + c2)

    def remote(src, dst, send, recv, device):
        return pltpu.make_async_remote_copy(
            src_ref=src, dst_ref=dst, send_sem=send, recv_sem=recv,
            device_id=device, device_id_type=MESH,
        )

    right, left, sibling = at(0, 0, 1, 0), at(0, 0, 3, 0), at(0, 0, 0, 1)
    others = [(dy, dz) for dz in (0, 1, 3, 2) for dy in (0, 1, 3, 2) if dy or dz]
    greeted = [at(dy, dz, 0, 0) for dy, dz in others] + [right, left, sibling]
    barrier = pltpu.get_barrier_semaphore()
    for device in greeted:
        pl.semaphore_signal(barrier, inc=1, device_id=device, device_id_type=MESH)
    pl.semaphore_wait(barrier, len(greeted))

    def lanes(first, size=HD):
        return pl.ds(pl.multiple_of(first, HD), size)

    my_rows = pl.ds(pl.multiple_of((y * 4 + z) * PAGE, PAGE), PAGE)
    page_copies = []
    n = 0
    for dy, dz in others:
        y2, z2 = lax.rem(y + dy, 4), lax.rem(z + dz, 4)
        for plane in range(2):
            page_copies.append(remote(
                pages.at[y2, :, lanes(plane * 512 + z2 * HD)],
                raw.at[plane, 0, c, my_rows],
                pg_send.at[n], pg_recv, at(dy, dz, 0, 0),
            ))
            n += 1
    for copy in page_copies:
        copy.start()
    own_pages = [
        pltpu.make_async_copy(
            pages.at[y, :, lanes(plane * 512 + z * HD)], raw.at[plane, 0, c, my_rows], pg_recv
        )
        for plane in range(2)
    ]
    for copy in own_pages:
        copy.start()

    own_q = pltpu.make_async_copy(queries.at[0, :, lanes(z * ROWS, ROWS)], q_raw.at[z], q_recv.at[0])
    own_q.start()
    xc = x * 2 + c
    fresh_copies = []
    n = 0
    for dz in (1, 3, 2):
        z2 = lax.rem(z + dz, 4)
        for plane in range(2):
            fresh_copies.append(remote(
                fresh.at[0, :, lanes(plane * 512 + z2 * HD)],
                kvx.at[plane, 4 + z, xc],
                fr_send.at[n], fr_recv, at(0, dz, 0, 0),
            ))
            n += 1
    for copy in fresh_copies:
        copy.start()
    own_fresh = [
        pltpu.make_async_copy(
            fresh.at[0, :, lanes(plane * 512 + z * HD)], kvx.at[plane, 4 + z, xc], fr_recv
        )
        for plane in range(2)
    ]
    for copy in own_fresh:
        copy.start()
    q_copies = {}
    for k, dz in enumerate((1, 3, 2)):
        z2 = lax.rem(z + dz, 4)
        k_there = {1: 2, 3: 1, 2: 3}[dz]
        q_copies[k] = remote(
            queries.at[0, :, lanes(z2 * ROWS, ROWS)], q_raw.at[z],
            q_send.at[k], q_recv.at[k_there], at(0, dz, 0, 0),
        )
        q_copies[k].start()
    written_copies = []
    for k, dy in enumerate((1, 2, 3)):
        y2 = lax.rem(y + dy, 4)
        written_copies.append(remote(
            fresh.at[0, pl.ds(pl.multiple_of(y2 * PAGE, PAGE), PAGE)], written.at[0, y, 0],
            np_send.at[k], np_recv, at(dy, 0, 0, 0),
        ))
    own_written = pltpu.make_async_copy(
        fresh.at[0, pl.ds(pl.multiple_of(y * PAGE, PAGE), PAGE)], written.at[0, y, 0], np_recv
    )

    length = lengths[y]
    j = lax.broadcasted_iota(jnp.int32, (128, 128), 0)
    rel = j // 32
    x_of = lax.rem(x + jnp.where(rel == 0, 0, jnp.where(rel == 1, 3, jnp.where(rel == 2, 1, 2))), 4)
    c_of = (j // 16) % 2
    y_of, z_of = (j // 4) % 4, j % 4
    slot = 4 * (y_of * 32 + z_of * 8 + x_of * 2 + c_of) + y
    page = lax.broadcasted_iota(jnp.int32, (128, 128), 1)
    match = jnp.broadcast_to(table[pl.ds(y, 1), :], (128, 128)) == slot
    place = jnp.sum(jnp.where(match, page, 0).astype(jnp.float32), axis=1, keepdims=True)
    limits[...] = jnp.broadcast_to(length.astype(jnp.float32) - PAGE * place, (128, 128))
    ones = jnp.ones((8, 128, 128), jnp.bfloat16)
    for chunk in range(4, 8):
        kvx[2, chunk] = ones

    def prepare_queries(i):
        for head in range(GROUP):
            block = q_raw[i, :, head * HD:(head + 1) * HD].astype(jnp.float32) * SCALE
            high = block.astype(jnp.bfloat16)
            low = (block - high.astype(jnp.float32)).astype(jnp.bfloat16)
            q_two[i, head * TOK:(head + 1) * TOK, 0:HD] = high
            q_two[i, head * TOK:(head + 1) * TOK, HD:2 * HD] = low

    def prepare_prefix(chunk):
        seen = kvx[0, 4, xc, 0:1, :].astype(jnp.float32)
        row = lax.broadcasted_iota(jnp.int32, (PAGE, 128), 0).astype(jnp.float32)

        def one_block(b, carry):
            for p in range(4):
                limit = limits[pl.ds(chunk * 32 + b * 4 + p, 1), :]
                valid = row < limit
                source = pl.ds(pl.multiple_of(lax.rem(b, 4) * 128 + p * PAGE, PAGE), PAGE)
                key = raw[0, chunk, b // 4, source, :].astype(jnp.float32)
                value = raw[1, chunk, b // 4, source, :].astype(jnp.float32)
                rows = pl.ds(p * PAGE, PAGE)
                kvx[0, chunk, b, rows, :] = jnp.where(valid, key, seen).astype(jnp.bfloat16)
                kvx[1, chunk, b, rows, :] = jnp.where(valid, value, 0.0).astype(jnp.bfloat16)
                kvx[2, chunk, b, rows, :] = jnp.where(valid, 1.0, 0.0).astype(jnp.bfloat16)
            return carry

        lax.fori_loop(0, 8, one_block, 0)

    def attend(i, chunk, count, first=False, diagonal=False):
        width = count * CHUNK

        def scores(r):
            key = kvx[0, pl.ds(chunk, count)].reshape(width, HD)
            two = jnp.concatenate([key, key], axis=1)
            return lax.dot_general(
                q_two[i, r:r + BLOCK, :], two, (((1,), (1,)), ((), ())),
                preferred_element_type=jnp.float32,
            )

        def absorb(r, s):
            if diagonal:
                token = lax.broadcasted_iota(jnp.int32, (BLOCK, CHUNK), 0) % TOK
                key_at = lax.broadcasted_iota(jnp.int32, (BLOCK, CHUNK), 1)
                cut = jnp.where(key_at - token <= xc * TOK, s[:, width - CHUNK:], NEG)
                s = cut if count == 1 else jnp.concatenate([s[:, :width - CHUNK], cut], axis=1)
            rows = slice(r, r + BLOCK)
            value = jnp.concatenate(
                [kvx[1, pl.ds(chunk, count)].reshape(width, HD), kvx[2, pl.ds(chunk, count)].reshape(width, HD)],
                axis=1,
            )
            highest = jnp.max(s, axis=1, keepdims=True)
            if not first:
                before = top[i, rows, :][:, :1]
                highest = jnp.maximum(before, highest)
            weights = jnp.exp2(s - highest).astype(jnp.bfloat16)
            top[i, rows, :] = jnp.broadcast_to(highest, (BLOCK, 128))
            added = jnp.dot(weights, value, preferred_element_type=jnp.float32)
            if first:
                acc[i, rows, :] = added
            else:
                acc[i, rows, :] = acc[i, rows, :] * jnp.exp2(before - highest) + added

        waiting = None
        for r in range(0, ROWS, BLOCK):
            s = scores(r)
            if waiting is not None:
                absorb(*waiting)
            waiting = (r, s)
        absorb(*waiting)

    sib_c = 1 - c
    del sib_c
    pre = lambda rel_x: raw.at[:, rel_x, c]
    low, high = pl.ds(0, 256), pl.ds(256, 256)
    xl, xr, xf = lax.rem(x + 3, 4), lax.rem(x + 1, 4), lax.rem(x + 2, 4)
    suf = lambda xs, part=pl.ds(4, 4): kvx.at[pl.ds(0, 2), part, xs * 2 + c]
    part_a, part_b = pl.ds(4, 2), pl.ds(6, 2)
    pre_plan = {
        "own_s": (pre(0), pre(0), 0, sibling),
        "own_r": (pre(0), pre(1), 1, right),
        "own_l": (pre(0), pre(2), 2, left),
        "far_r": (raw.at[:, 1, c, low], raw.at[:, 3, c, low], 3, right),
        "far_l": (raw.at[:, 2, c, high], raw.at[:, 3, c, high], 4, left),
        "left_s": (pre(1), pre(1), 5, sibling),
        "right_s": (pre(2), pre(2), 6, sibling),
        "fara_s": (raw.at[:, 3, c, low], raw.at[:, 3, c, low], 7, sibling),
        "farb_s": (raw.at[:, 3, c, high], raw.at[:, 3, c, high], 8, sibling),
    }
    suf_plan = {
        "own_s": (suf(x), suf(x), 0, sibling),
        "own_r": (suf(x), suf(x), 1, right),
        "own_l": (suf(x), suf(x), 2, left),
        "far_r": (suf(xl, part_a), suf(xl, part_a), 3, right),
        "far_l": (suf(xr, part_b), suf(xr, part_b), 4, left),
        "left_s": (suf(xl), suf(xl), 5, sibling),
        "right_s": (suf(xr), suf(xr), 6, sibling),
        "fara_s": (suf(xf, part_a), suf(xf, part_a), 7, sibling),
        "farb_s": (suf(xf, part_b), suf(xf, part_b), 8, sibling),
    }

    def pre_copy(name):
        src, dst, number, device = pre_plan[name]
        return remote(src, dst, pre_send.at[number], pre_recv.at[number], device)

    def suf_copy(name):
        src, dst, number, device = suf_plan[name]
        return remote(src, dst, suf_send.at[number], suf_recv.at[number], device)

    own_q.wait()
    prepare_queries(z)
    own_slot = raw.at[:, 0, c]
    pltpu.make_async_copy(own_slot, own_slot, pg_recv).wait()
    for name in ("own_r", "own_l", "own_s"):
        pre_copy(name).start()
    own_new = kvx.at[pl.ds(0, 2), pl.ds(4, 4), xc]
    pltpu.make_async_copy(own_new, own_new, fr_recv).wait()
    for name in ("own_r", "own_l", "own_s"):
        suf_copy(name).start()
    pre_copy("own_s").wait_recv()
    prepare_prefix(0)

    def wait_queries(k, i):
        pltpu.make_async_copy(q_raw.at[i], q_raw.at[i], q_recv.at[k]).wait()
        prepare_queries(i)

    def order(k):
        return lax.rem(z + jnp.where(k < 2, k, 5 - k), 4)

    def phase_a(k, carry):
        i = order(k)

        @pl.when(k > 0)
        def _():
            wait_queries(k, i)

        attend(i, 0, 1, first=True)

        @pl.when(k == 2)
        def _():
            pre_copy("own_r").wait_recv()
            pre_copy("far_r").start()
            pre_copy("left_s").start()
            pre_copy("own_l").wait_recv()
            pre_copy("far_l").start()
            pre_copy("right_s").start()

        return carry

    lax.fori_loop(0, 4, phase_a, 0)
    for copy in written_copies:
        copy.start()
    own_written.start()
    pre_copy("left_s").wait_recv()
    pre_copy("right_s").wait_recv()
    prepare_prefix(1)
    prepare_prefix(2)

    def phase_b(k, carry):
        attend(order(k), 1, 2)

        @pl.when(k == 0)
        def _():
            pre_copy("far_r").wait_recv()
            pre_copy("fara_s").start()
            pre_copy("far_l").wait_recv()
            pre_copy("farb_s").start()

        @pl.when(k == 1)
        def _():
            suf_copy("own_r").wait_recv()
            suf_copy("far_r").start()
            suf_copy("left_s").start()
            suf_copy("own_l").wait_recv()
            suf_copy("far_l").start()
            suf_copy("right_s").start()

        @pl.when(k == 3)
        def _():
            suf_copy("far_r").wait_recv()
            suf_copy("fara_s").start()
            suf_copy("far_l").wait_recv()
            suf_copy("farb_s").start()

        return carry

    lax.fori_loop(0, 4, phase_b, 0)
    for name in ("fara_s", "farb_s"):
        pre_copy(name).wait_recv()
    prepare_prefix(3)
    for name in ("own_s", "left_s", "right_s", "fara_s", "farb_s"):
        suf_copy(name).wait_recv()

    def out_copy(i):
        return remote(
            o_buf.at[i], attended.at[0, :, lanes(z * ROWS, ROWS)], o_send.at[i], o_recv, (y, i * 8 + xc)
        )

    def own_out():
        return pltpu.make_async_copy(o_buf.at[z], attended.at[0, :, lanes(z * ROWS, ROWS)], o_recv)

    def phase_c(k, carry):
        i = lax.rem(z + jnp.where(k == 0, 2, jnp.where(k == 1, 1, jnp.where(k == 2, 3, 0))), 4)

        @pl.when(i == 0)
        def _():
            attend(i, 3, 2, diagonal=True)

        @pl.when(i > 0)
        def _():
            lax.fori_loop(0, jnp.where(i == 3, 2, 1), lambda t, u: (attend(i, 3 + 2 * t, 2), u)[1], 0)

        @pl.when(i == 2)
        def _():
            attend(i, 5, 2, diagonal=True)

        @pl.when(lax.rem(i, 2) == 1)
        def _():
            attend(i, 4 + i, 1, diagonal=True)

        for head in range(GROUP):
            rows = slice(head * TOK, (head + 1) * TOK)
            o_buf[i, :, head * HD:(head + 1) * HD] = (
                acc[i, rows, 0:HD] / acc[i, rows, HD:2 * HD]
            ).astype(jnp.bfloat16)

        @pl.when(k < 3)
        def _():
            out_copy(i).start()

        @pl.when(k == 3)
        def _():
            own_out().start()

        return carry

    lax.fori_loop(0, 4, phase_c, 0)

    for copy in page_copies + fresh_copies + list(q_copies.values()) + written_copies:
        copy.wait_send()
    for name in pre_plan:
        pre_copy(name).wait_send()
        suf_copy(name).wait_send()
    pltpu.make_async_copy(written, written, np_recv).wait()
    for dz in (1, 3, 2):
        out_copy(lax.rem(z + dz, 4)).wait_send()
    pltpu.make_async_copy(attended, attended, o_recv).wait()


def per_device(queries, fresh_cache, page_store, page_table, prefix_lengths):
    anywhere = pl.BlockSpec(memory_space=pl.ANY)
    bf16, f32 = jnp.bfloat16, jnp.float32
    dma = pltpu.SemaphoreType.DMA
    return pl.pallas_call(
        kernel,
        out_shape=(
            jax.ShapeDtypeStruct((1, TOK, H * HD), bf16),
            jax.ShapeDtypeStruct((1, 4, 1, PAGE, 2 * KVH * HD), bf16),
        ),
        in_specs=[
            anywhere, anywhere, anywhere,
            pl.BlockSpec(memory_space=pltpu.VMEM),
            pl.BlockSpec(memory_space=pltpu.SMEM),
        ],
        out_specs=(anywhere, anywhere),
        scratch_shapes=[
            pltpu.VMEM((3, 8, 8, 128, HD), bf16),
            pltpu.VMEM((2, 4, 2, 512, HD), bf16),
            pltpu.VMEM((4, TOK, ROWS), bf16),
            pltpu.VMEM((4, ROWS, 2 * HD), bf16),
            pltpu.VMEM((4, ROWS, 2 * HD), f32),
            pltpu.VMEM((4, ROWS, 128), f32),
            pltpu.VMEM((4, TOK, ROWS), bf16),
            pltpu.VMEM((128, 128), f32),
            dma((30,)), dma, dma((6,)), dma, dma((3,)), dma((4,)), dma((4,)), dma,
            dma((3,)), dma, dma((9,)), dma((9,)), dma((9,)), dma((9,)),
        ],
        compiler_params=pltpu.CompilerParams(
            collective_id=0, has_side_effects=True, vmem_limit_bytes=56 * 2**20
        ),
        cost_estimate=pl.CostEstimate(flops=2 * 2 * 4096 * 6656 * 128, bytes_accessed=4 * 2**20, transcendentals=4096 * 6656),
    )(queries, fresh_cache, page_store, page_table, prefix_lengths)


def solution(mesh):
    placed = (P("req", "blk", None), P("req", "blk", None), P(("req", "blk"), None, None), P(), P())
    return jax.shard_map(
        per_device,
        mesh=mesh,
        in_specs=placed,
        out_specs=(P("req", "blk", None), P("req", None, "blk", None, None)),
        check_vma=False,
    )
```

```python
import functools
import math

import jax
import jax.numpy as jnp
from jax import lax
from jax.experimental import pallas as pl
from jax.experimental.pallas import tpu as pltpu
from jax.sharding import PartitionSpec as P

H = 32
KVH = 4
HD = 128
GROUP = H // KVH
TOK = 128
PAGE = 32
CHUNK = 1024
ROWS = GROUP * TOK
NEG = -1e30
SCALE = math.log2(math.e) / math.sqrt(HD)
MESH = pl.DeviceIdType.MESH
BLOCK = 256


def kernel(
    queries, fresh, pages, table, lengths, attended, written,
    kvx, raw, q_raw, q_two, acc, top, o_buf, limits,
    paged, py_send, py_recv, pg_send, pg_recv, fr_send, fr_recv, q_send, q_recv, o_send, o_recv,
    np_send, np_recv, pre_send, pre_recv, suf_send, suf_recv,
):
    y = lax.axis_index("req")
    blk = lax.axis_index("blk")
    z, x, c = blk // 8, (blk // 2) % 4, blk % 2

    def at(dy, dz, dx, dc):
        z2, x2 = lax.rem(z + dz, 4), lax.rem(x + dx, 4)
        c2 = 1 - c if dc else c
        return (lax.rem(y + dy, 4), z2 * 8 + x2 * 2 + c2)

    def remote(src, dst, send, recv, device):
        return pltpu.make_async_remote_copy(
            src_ref=src, dst_ref=dst, send_sem=send, recv_sem=recv,
            device_id=device, device_id_type=MESH,
        )

    right, left, sibling = at(0, 0, 1, 0), at(0, 0, 3, 0), at(0, 0, 0, 1)
    greeted = [at(dy, 0, 0, 0) for dy in (1, 3, 2)] + [at(0, dz, 0, 0) for dz in (1, 3, 2)]
    greeted += [right, left, sibling]
    barrier = pltpu.get_barrier_semaphore()
    for device in greeted:
        pl.semaphore_signal(barrier, inc=1, device_id=device, device_id_type=MESH)

    def lanes(first, size=HD):
        return pl.ds(pl.multiple_of(first, HD), size)

    def page_rows(first):
        return pl.ds(pl.multiple_of(first * PAGE, PAGE), PAGE)

    xc = x * 2 + c
    slab = pl.ds(pl.multiple_of(z * TOK, TOK), TOK)
    page_copies, slab_copies, fresh_copies, written_copies = [], [], [], []
    for k, dy in enumerate((1, 3, 2)):
        y2 = lax.rem(y + dy, 4)
        page_copies.append(remote(
            pages.at[y2], paged.at[page_rows(y)], py_send.at[k], py_recv, at(dy, 0, 0, 0)
        ))
        written_copies.append(remote(
            fresh.at[0, page_rows(y2)], written.at[0, y, 0], np_send.at[k], np_recv, at(dy, 0, 0, 0)
        ))
    own_page = pltpu.make_async_copy(pages.at[y], paged.at[page_rows(y)], py_recv)
    own_written = pltpu.make_async_copy(fresh.at[0, page_rows(y)], written.at[0, y, 0], np_recv)
    q_copies = []
    for k, dz in enumerate((1, 3, 2)):
        z2 = lax.rem(z + dz, 4)
        for plane in range(2):
            head = lanes(plane * 512 + z2 * HD)
            slab_copies.append(remote(
                paged.at[:, head], raw.at[plane, 0, c, slab], pg_send.at[2 * k + plane], pg_recv, at(0, dz, 0, 0)
            ))
            fresh_copies.append(remote(
                fresh.at[0, :, head], kvx.at[plane, 4 + z, xc], fr_send.at[2 * k + plane], fr_recv, at(0, dz, 0, 0)
            ))
        k_there = {1: 2, 3: 1, 2: 3}[dz]
        q_copies.append(remote(
            queries.at[0, :, lanes(z2 * ROWS, ROWS)], q_raw.at[z],
            q_send.at[k], q_recv.at[k_there], at(0, dz, 0, 0),
        ))
    own_slab, own_fresh = [], []
    for plane in range(2):
        head = lanes(plane * 512 + z * HD)
        own_slab.append(pltpu.make_async_copy(paged.at[:, head], raw.at[plane, 0, c, slab], pg_recv))
        own_fresh.append(pltpu.make_async_copy(fresh.at[0, :, head], kvx.at[plane, 4 + z, xc], fr_recv))
    own_q = pltpu.make_async_copy(queries.at[0, :, lanes(z * ROWS, ROWS)], q_raw.at[z], q_recv.at[0])
    for copy in [own_q, own_page] + own_fresh:
        copy.start()

    length = lengths[y]
    j = lax.broadcasted_iota(jnp.int32, (128, 128), 0)
    rel = j // 32
    x_of = lax.rem(x + jnp.where(rel == 0, 0, jnp.where(rel == 1, 3, jnp.where(rel == 2, 1, 2))), 4)
    c_of = (j // 16) % 2
    z_of, y_of = (j // 4) % 4, j % 4
    slot = 4 * (y_of * 32 + z_of * 8 + x_of * 2 + c_of) + y
    page = lax.broadcasted_iota(jnp.int32, (128, 128), 1)
    match = jnp.broadcast_to(table[pl.ds(y, 1), :], (128, 128)) == slot
    place = jnp.sum(jnp.where(match, page, 0).astype(jnp.float32), axis=1, keepdims=True)
    limits[...] = jnp.broadcast_to(length.astype(jnp.float32) - PAGE * place, (128, 128))
    ones = jnp.ones((8, 128, 128), jnp.bfloat16)
    for chunk in range(4, 8):
        kvx[2, chunk] = ones

    def prepare_queries(i):
        for head in range(GROUP):
            block = q_raw[i, :, head * HD:(head + 1) * HD].astype(jnp.float32) * SCALE
            high = block.astype(jnp.bfloat16)
            low = (block - high.astype(jnp.float32)).astype(jnp.bfloat16)
            q_two[i, head * TOK:(head + 1) * TOK, 0:HD] = high
            q_two[i, head * TOK:(head + 1) * TOK, HD:2 * HD] = low

    def prepare_prefix(chunk):
        seen = kvx[0, 4, xc, 0:1, :].astype(jnp.float32)
        row = lax.broadcasted_iota(jnp.int32, (PAGE, 128), 0).astype(jnp.float32)

        def one_block(b, carry):
            for p in range(4):
                limit = limits[pl.ds(chunk * 32 + b * 4 + p, 1), :]
                valid = row < limit
                source = pl.ds(pl.multiple_of(lax.rem(b, 4) * 128 + p * PAGE, PAGE), PAGE)
                key = raw[0, chunk, b // 4, source, :].astype(jnp.float32)
                value = raw[1, chunk, b // 4, source, :].astype(jnp.float32)
                rows = pl.ds(p * PAGE, PAGE)
                kvx[0, chunk, b, rows, :] = jnp.where(valid, key, seen).astype(jnp.bfloat16)
                kvx[1, chunk, b, rows, :] = jnp.where(valid, value, 0.0).astype(jnp.bfloat16)
                kvx[2, chunk, b, rows, :] = jnp.where(valid, 1.0, 0.0).astype(jnp.bfloat16)
            return carry

        lax.fori_loop(0, 8, one_block, 0)

    def attend(i, chunk, count, first=False, diagonal=False):
        width = count * CHUNK

        def scores(r):
            key = kvx[0, pl.ds(chunk, count)].reshape(width, HD)
            two = jnp.concatenate([key, key], axis=1)
            return lax.dot_general(
                q_two[i, r:r + BLOCK, :], two, (((1,), (1,)), ((), ())),
                preferred_element_type=jnp.float32,
            )

        def absorb(r, s):
            if diagonal:
                token = lax.broadcasted_iota(jnp.int32, (BLOCK, CHUNK), 0) % TOK
                key_at = lax.broadcasted_iota(jnp.int32, (BLOCK, CHUNK), 1)
                cut = jnp.where(key_at - token <= xc * TOK, s[:, width - CHUNK:], NEG)
                s = cut if count == 1 else jnp.concatenate([s[:, :width - CHUNK], cut], axis=1)
            rows = slice(r, r + BLOCK)
            value = jnp.concatenate(
                [kvx[1, pl.ds(chunk, count)].reshape(width, HD), kvx[2, pl.ds(chunk, count)].reshape(width, HD)],
                axis=1,
            )
            highest = jnp.max(s, axis=1, keepdims=True)
            if not first:
                before = top[i, rows, :][:, :1]
                highest = jnp.maximum(before, highest)
            weights = jnp.exp2(s - highest).astype(jnp.bfloat16)
            top[i, rows, :] = jnp.broadcast_to(highest, (BLOCK, 128))
            added = jnp.dot(weights, value, preferred_element_type=jnp.float32)
            if first:
                acc[i, rows, :] = added
            else:
                acc[i, rows, :] = acc[i, rows, :] * jnp.exp2(before - highest) + added

        waiting = None
        for r in range(0, ROWS, BLOCK):
            s = scores(r)
            if waiting is not None:
                absorb(*waiting)
            waiting = (r, s)
        absorb(*waiting)

    pre = lambda rel_x: raw.at[:, rel_x, c]
    low, high = pl.ds(0, 256), pl.ds(256, 256)
    xl, xr, xf = lax.rem(x + 3, 4), lax.rem(x + 1, 4), lax.rem(x + 2, 4)
    suf = lambda xs, part=pl.ds(4, 4): kvx.at[pl.ds(0, 2), part, xs * 2 + c]
    part_a, part_b = pl.ds(4, 2), pl.ds(6, 2)
    pre_plan = {
        "own_s": (pre(0), pre(0), 0, sibling),
        "own_r": (pre(0), pre(1), 1, right),
        "own_l": (pre(0), pre(2), 2, left),
        "far_r": (raw.at[:, 1, c, low], raw.at[:, 3, c, low], 3, right),
        "far_l": (raw.at[:, 2, c, high], raw.at[:, 3, c, high], 4, left),
        "left_s": (pre(1), pre(1), 5, sibling),
        "right_s": (pre(2), pre(2), 6, sibling),
        "fara_s": (raw.at[:, 3, c, low], raw.at[:, 3, c, low], 7, sibling),
        "farb_s": (raw.at[:, 3, c, high], raw.at[:, 3, c, high], 8, sibling),
    }
    suf_plan = {
        "own_s": (suf(x), suf(x), 0, sibling),
        "own_r": (suf(x), suf(x), 1, right),
        "own_l": (suf(x), suf(x), 2, left),
        "far_r": (suf(xl, part_a), suf(xl, part_a), 3, right),
        "far_l": (suf(xr, part_b), suf(xr, part_b), 4, left),
        "left_s": (suf(xl), suf(xl), 5, sibling),
        "right_s": (suf(xr), suf(xr), 6, sibling),
        "fara_s": (suf(xf, part_a), suf(xf, part_a), 7, sibling),
        "farb_s": (suf(xf, part_b), suf(xf, part_b), 8, sibling),
    }

    def pre_copy(name):
        src, dst, number, device = pre_plan[name]
        return remote(src, dst, pre_send.at[number], pre_recv.at[number], device)

    def suf_copy(name):
        src, dst, number, device = suf_plan[name]
        return remote(src, dst, suf_send.at[number], suf_recv.at[number], device)

    def wait_queries(k, i):
        pltpu.make_async_copy(q_raw.at[i], q_raw.at[i], q_recv.at[k]).wait()
        prepare_queries(i)

    own_q.wait()
    prepare_queries(z)
    pl.semaphore_wait(barrier, len(greeted))
    for copy in page_copies + q_copies[:2]:
        copy.start()
    pltpu.make_async_copy(paged, paged, py_recv).wait()
    for copy in slab_copies + own_slab:
        copy.start()
    own_slot = raw.at[:, 0, c]
    pltpu.make_async_copy(own_slot, own_slot, pg_recv).wait()
    for name in ("own_r", "own_l", "own_s"):
        pre_copy(name).start()
    for copy in fresh_copies:
        copy.start()
    own_new = kvx.at[pl.ds(0, 2), pl.ds(4, 4), xc]
    pltpu.make_async_copy(own_new, own_new, fr_recv).wait()
    for name in ("own_r", "own_l", "own_s"):
        suf_copy(name).start()
    for copy in [q_copies[2], own_written] + written_copies:
        copy.start()
    pre_copy("own_s").wait_recv()
    prepare_prefix(0)

    def order(k):
        return lax.rem(z + jnp.where(k < 2, k, 5 - k), 4)

    def phase_a(k, carry):
        i = order(k)

        @pl.when(k > 0)
        def _():
            wait_queries(k, i)

        attend(i, 0, 1, first=True)
        return carry

    lax.fori_loop(0, 3, phase_a, 0)
    pre_copy("own_r").wait_recv()
    pre_copy("far_r").start()
    pre_copy("left_s").start()
    pre_copy("own_l").wait_recv()
    pre_copy("far_l").start()
    pre_copy("right_s").start()
    pre_copy("left_s").wait_recv()
    prepare_prefix(1)
    pre_copy("right_s").wait_recv()
    prepare_prefix(2)

    def phase_b(k, carry):
        @pl.when(k < 3)
        def _():
            attend(lax.rem(z + jnp.where(k == 0, 1, jnp.where(k == 1, 3, 0)), 4), 1, 2)

        @pl.when(k == 0)
        def _():
            pre_copy("far_r").wait_recv()
            pre_copy("fara_s").start()
            pre_copy("far_l").wait_recv()
            pre_copy("farb_s").start()

        @pl.when(k == 1)
        def _():
            suf_copy("own_r").wait_recv()
            suf_copy("far_r").start()
            suf_copy("left_s").start()
            suf_copy("own_l").wait_recv()
            suf_copy("far_l").start()
            suf_copy("right_s").start()

        @pl.when(k == 3)
        def _():
            i = lax.rem(z + 2, 4)
            wait_queries(3, i)
            attend(i, 0, 3, first=True)
            suf_copy("far_r").wait_recv()
            suf_copy("fara_s").start()
            suf_copy("far_l").wait_recv()
            suf_copy("farb_s").start()

        return carry

    lax.fori_loop(0, 4, phase_b, 0)
    for name in ("fara_s", "farb_s"):
        pre_copy(name).wait_recv()
    prepare_prefix(3)
    for name in ("own_s", "left_s", "right_s", "fara_s", "farb_s"):
        suf_copy(name).wait_recv()

    def out_copy(i):
        return remote(
            o_buf.at[i], attended.at[0, :, lanes(z * ROWS, ROWS)], o_send.at[i], o_recv, (y, i * 8 + xc)
        )

    def own_out():
        return pltpu.make_async_copy(o_buf.at[z], attended.at[0, :, lanes(z * ROWS, ROWS)], o_recv)

    def phase_c(k, carry):
        i = lax.rem(z + jnp.where(k == 0, 2, jnp.where(k == 1, 1, jnp.where(k == 2, 3, 0))), 4)

        @pl.when(i == 0)
        def _():
            attend(i, 3, 2, diagonal=True)

        @pl.when(i == 3)
        def _():
            attend(i, 3, 2)

        @pl.when(lax.rem(i, 2) == 1)
        def _():
            attend(i, 2 + i, 3, diagonal=True)

        @pl.when(i == 2)
        def _():
            attend(i, 3, 4, diagonal=True)

        for head in range(GROUP):
            rows = slice(head * TOK, (head + 1) * TOK)
            o_buf[i, :, head * HD:(head + 1) * HD] = (
                acc[i, rows, 0:HD] / acc[i, rows, HD:2 * HD]
            ).astype(jnp.bfloat16)

        @pl.when(k < 3)
        def _():
            out_copy(i).start()

        @pl.when(k == 3)
        def _():
            own_out().start()

        return carry

    lax.fori_loop(0, 4, phase_c, 0)

    for copy in page_copies + slab_copies + fresh_copies + q_copies + written_copies:
        copy.wait_send()
    for name in pre_plan:
        pre_copy(name).wait_send()
        suf_copy(name).wait_send()
    pltpu.make_async_copy(written, written, np_recv).wait()
    for dz in (1, 3, 2):
        out_copy(lax.rem(z + dz, 4)).wait_send()
    pltpu.make_async_copy(attended, attended, o_recv).wait()


def hand_over(attended_in, written_in, attended, written, sems):
    rows = [pl.ds(32 * k, 32) for k in range(4)]
    copies = [
        pltpu.make_async_copy(attended_in.at[0, part], attended.at[0, part], sems.at[k])
        for k, part in enumerate(rows)
    ]
    copies.append(pltpu.make_async_copy(written_in, written, sems.at[4]))
    for copy in copies:
        copy.start()
    for copy in copies:
        copy.wait()


def per_device(queries, fresh_cache, page_store, page_table, prefix_lengths):
    anywhere = pl.BlockSpec(memory_space=pl.ANY)
    bf16, f32 = jnp.bfloat16, jnp.float32
    dma = pltpu.SemaphoreType.DMA
    outs_shape = (
        jax.ShapeDtypeStruct((1, TOK, H * HD), bf16),
        jax.ShapeDtypeStruct((1, 4, 1, PAGE, 2 * KVH * HD), bf16),
    )
    outs = pl.pallas_call(
        kernel,
        out_shape=outs_shape,
        in_specs=[
            anywhere, anywhere, anywhere,
            pl.BlockSpec(memory_space=pltpu.VMEM),
            pl.BlockSpec(memory_space=pltpu.SMEM),
        ],
        out_specs=(anywhere, anywhere),
        scratch_shapes=[
            pltpu.VMEM((3, 8, 8, 128, HD), bf16),
            pltpu.VMEM((2, 4, 2, 512, HD), bf16),
            pltpu.VMEM((4, TOK, ROWS), bf16),
            pltpu.VMEM((4, ROWS, 2 * HD), bf16),
            pltpu.VMEM((4, ROWS, 2 * HD), f32),
            pltpu.VMEM((4, ROWS, 128), f32),
            pltpu.VMEM((4, TOK, ROWS), bf16),
            pltpu.VMEM((128, 128), f32),
            pltpu.VMEM((4 * PAGE, 2 * KVH * HD), bf16),
            dma((3,)), dma, dma((6,)), dma, dma((6,)), dma, dma((3,)), dma((4,)), dma((4,)), dma,
            dma((3,)), dma, dma((9,)), dma((9,)), dma((9,)), dma((9,)),
        ],
        compiler_params=pltpu.CompilerParams(
            collective_id=0, has_side_effects=True, vmem_limit_bytes=56 * 2**20
        ),
        cost_estimate=pl.CostEstimate(flops=2 * 2 * 4096 * 6656 * 128, bytes_accessed=4 * 2**20, transcendentals=4096 * 6656),
    )(queries, fresh_cache, page_store, page_table, prefix_lengths)
    return pl.pallas_call(
        hand_over,
        out_shape=outs_shape,
        in_specs=[anywhere, anywhere],
        out_specs=(anywhere, anywhere),
        scratch_shapes=[dma((5,))],
    )(*outs)


def solution(mesh):
    placed = (P("req", "blk", None), P("req", "blk", None), P(("req", "blk"), None, None), P(), P())
    return jax.shard_map(
        per_device,
        mesh=mesh,
        in_specs=placed,
        out_specs=(P("req", "blk", None), P("req", None, "blk", None, None)),
        check_vma=False,
    )
```

```python
import functools
import math

import jax
import jax.numpy as jnp
from jax import lax
from jax.experimental import pallas as pl
from jax.experimental.pallas import tpu as pltpu
from jax.sharding import PartitionSpec as P

H = 32
KVH = 4
HD = 128
GROUP = H // KVH
TOK = 128
PAGE = 32
CHUNK = 1024
ROWS = GROUP * TOK
HALF = ROWS // 2
NEG = -1e30
SCALE = math.log2(math.e) / math.sqrt(HD)
MESH = pl.DeviceIdType.MESH
BLOCK = 256


def kernel(
    queries, fresh, pages, table, lengths, attended, written,
    kvx, raw, q_raw, q_two, acc, top, o_buf, limits,
    paged, seen_key, se_send, se_recv, py_send, py_recv, pg_send, pg_recv, fr_send, fr_recv, q_send, q_recv, o_send, o_recv,
    np_send, np_recv, pre_send, pre_recv, suf_send, suf_recv,
):
    y = lax.axis_index("req")
    blk = lax.axis_index("blk")
    z, x, c = blk // 8, (blk // 2) % 4, blk % 2

    def at(dy, dz, dx, dc):
        z2, x2 = lax.rem(z + dz, 4), lax.rem(x + dx, 4)
        c2 = 1 - c if dc else c
        return (lax.rem(y + dy, 4), z2 * 8 + x2 * 2 + c2)

    def remote(src, dst, send, recv, device):
        return pltpu.make_async_remote_copy(
            src_ref=src, dst_ref=dst, send_sem=send, recv_sem=recv,
            device_id=device, device_id_type=MESH,
        )

    right, left, sibling = at(0, 0, 1, 0), at(0, 0, 3, 0), at(0, 0, 0, 1)
    greeted = [at(dy, 0, 0, 0) for dy in (1, 3, 2)] + [at(0, dz, 0, 0) for dz in (1, 3, 2)]
    greeted += [right, left, sibling]
    barrier = pltpu.get_barrier_semaphore()
    for device in greeted:
        pl.semaphore_signal(barrier, inc=1, device_id=device, device_id_type=MESH)

    def lanes(first, size=HD):
        return pl.ds(pl.multiple_of(first, HD), size)

    def page_rows(first):
        return pl.ds(pl.multiple_of(first * PAGE, PAGE), PAGE)

    xc = x * 2 + c
    slab = pl.ds(pl.multiple_of(z * TOK, TOK), TOK)
    page_copies, slab_copies, fresh_copies, written_copies = [], [], [], []
    for k, dy in enumerate((1, 3, 2)):
        y2 = lax.rem(y + dy, 4)
        page_copies.append(remote(
            pages.at[y2], paged.at[page_rows(y)], py_send.at[k], py_recv, at(dy, 0, 0, 0)
        ))
        written_copies.append(remote(
            fresh.at[0, page_rows(y2)], written.at[0, y, 0], np_send.at[k], np_recv, at(dy, 0, 0, 0)
        ))
    own_page = pltpu.make_async_copy(pages.at[y], paged.at[page_rows(y)], py_recv)
    own_written = pltpu.make_async_copy(fresh.at[0, page_rows(y)], written.at[0, y, 0], np_recv)
    q_copies, seen_copies = [], []
    for k, dz in enumerate((1, 3, 2)):
        z2 = lax.rem(z + dz, 4)
        for plane in range(2):
            head = lanes(plane * 512 + z2 * HD)
            slab_copies.append(remote(
                paged.at[:, head], raw.at[plane, 0, c, slab], pg_send.at[2 * k + plane], pg_recv, at(0, dz, 0, 0)
            ))
            fresh_copies.append(remote(
                fresh.at[0, :, head], kvx.at[plane, 4 + z, xc], fr_send.at[2 * k + plane], fr_recv, at(0, dz, 0, 0)
            ))
        if dz == 2:
            q_far = remote(
                queries.at[0, :, lanes(z2 * ROWS, ROWS)], q_raw.at[z], q_send.at[4], q_recv.at[5], at(0, dz, 0, 0)
            )
        else:
            for half in range(2):
                q_copies.append(remote(
                    queries.at[0, :, lanes(z2 * ROWS + half * HALF, HALF)],
                    q_raw.at[z, :, half * HALF:(half + 1) * HALF],
                    q_send.at[2 * k + half], q_recv.at[{1: 3, 3: 1}[dz] + half], at(0, dz, 0, 0),
                ))
        seen_copies.append(remote(
            fresh.at[0, 0:16, lanes(z2 * HD)], seen_key, se_send.at[k], se_recv, at(0, dz, 0, 0)
        ))
    own_seen = pltpu.make_async_copy(fresh.at[0, 0:16, lanes(z * HD)], seen_key, se_recv)
    own_slab, own_fresh = [], []
    for plane in range(2):
        head = lanes(plane * 512 + z * HD)
        own_slab.append(pltpu.make_async_copy(paged.at[:, head], raw.at[plane, 0, c, slab], pg_recv))
        own_fresh.append(pltpu.make_async_copy(fresh.at[0, :, head], kvx.at[plane, 4 + z, xc], fr_recv))
    own_q = pltpu.make_async_copy(queries.at[0, :, lanes(z * ROWS, ROWS)], q_raw.at[z], q_recv.at[0])
    for copy in [own_q, own_page] + own_fresh:
        copy.start()

    length = lengths[y]
    j = lax.broadcasted_iota(jnp.int32, (128, 128), 0)
    rel = j // 32
    x_of = lax.rem(x + jnp.where(rel == 0, 0, jnp.where(rel == 1, 3, jnp.where(rel == 2, 1, 2))), 4)
    c_of = (j // 16) % 2
    z_of, y_of = (j // 4) % 4, j % 4
    slot = 4 * (y_of * 32 + z_of * 8 + x_of * 2 + c_of) + y
    page = lax.broadcasted_iota(jnp.int32, (128, 128), 1)
    match = jnp.broadcast_to(table[pl.ds(y, 1), :], (128, 128)) == slot
    place = jnp.sum(jnp.where(match, page, 0).astype(jnp.float32), axis=1, keepdims=True)
    limits[...] = jnp.broadcast_to(length.astype(jnp.float32) - PAGE * place, (128, 128))
    ones = jnp.ones((8, 128, 128), jnp.bfloat16)
    for chunk in range(4, 8):
        kvx[2, chunk] = ones

    def prepare_queries(i, first=0, last=GROUP):
        for head in range(first, last):
            block = q_raw[i, :, head * HD:(head + 1) * HD].astype(jnp.float32) * SCALE
            high = block.astype(jnp.bfloat16)
            low = (block - high.astype(jnp.float32)).astype(jnp.bfloat16)
            q_two[i, head * TOK:(head + 1) * TOK, 0:HD] = high
            q_two[i, head * TOK:(head + 1) * TOK, HD:2 * HD] = low

    def prepare_prefix(chunk):
        seen = seen_key[...].astype(jnp.float32)[0:1, :]
        row = lax.broadcasted_iota(jnp.int32, (PAGE, 128), 0).astype(jnp.float32)

        def one_block(b, carry):
            for p in range(4):
                limit = limits[pl.ds(chunk * 32 + b * 4 + p, 1), :]
                valid = row < limit
                source = pl.ds(pl.multiple_of(lax.rem(b, 4) * 128 + p * PAGE, PAGE), PAGE)
                key = raw[0, chunk, b // 4, source, :].astype(jnp.float32)
                value = raw[1, chunk, b // 4, source, :].astype(jnp.float32)
                rows = pl.ds(p * PAGE, PAGE)
                kvx[0, chunk, b, rows, :] = jnp.where(valid, key, seen).astype(jnp.bfloat16)
                kvx[1, chunk, b, rows, :] = jnp.where(valid, value, 0.0).astype(jnp.bfloat16)
                kvx[2, chunk, b, rows, :] = jnp.where(valid, 1.0, 0.0).astype(jnp.bfloat16)
            return carry

        lax.fori_loop(0, 8, one_block, 0)

    def attend(i, chunk, count, first=False, diagonal=False, blocks=None):
        blocks = blocks or [(i, slice(r, r + BLOCK)) for r in range(0, ROWS, BLOCK)]
        width = count * CHUNK

        def scores(i, rows):
            key = kvx[0, pl.ds(chunk, count)].reshape(width, HD)
            two = jnp.concatenate([key, key], axis=1)
            return lax.dot_general(
                q_two[i, rows, :], two, (((1,), (1,)), ((), ())),
                preferred_element_type=jnp.float32,
            )

        def absorb(i, rows, s):
            if diagonal:
                token = lax.broadcasted_iota(jnp.int32, (BLOCK, CHUNK), 0) % TOK
                key_at = lax.broadcasted_iota(jnp.int32, (BLOCK, CHUNK), 1)
                cut = jnp.where(key_at - token <= xc * TOK, s[:, width - CHUNK:], NEG)
                s = cut if count == 1 else jnp.concatenate([s[:, :width - CHUNK], cut], axis=1)
            value = jnp.concatenate(
                [kvx[1, pl.ds(chunk, count)].reshape(width, HD), kvx[2, pl.ds(chunk, count)].reshape(width, HD)],
                axis=1,
            )
            highest = jnp.max(s, axis=1, keepdims=True)
            if not first:
                before = top[i, rows, :][:, :1]
                highest = jnp.maximum(before, highest)
            weights = jnp.exp2(s - highest).astype(jnp.bfloat16)
            top[i, rows, :] = jnp.broadcast_to(highest, (BLOCK, 128))
            added = jnp.dot(weights, value, preferred_element_type=jnp.float32)
            if first:
                acc[i, rows, :] = added
            else:
                acc[i, rows, :] = acc[i, rows, :] * jnp.exp2(before - highest) + added

        waiting = None
        for i, rows in blocks:
            s = scores(i, rows)
            if waiting is not None:
                absorb(*waiting)
            waiting = (i, rows, s)
        absorb(*waiting)

    pre = lambda rel_x: raw.at[:, rel_x, c]
    low, high = pl.ds(0, 256), pl.ds(256, 256)
    xl, xr, xf = lax.rem(x + 3, 4), lax.rem(x + 1, 4), lax.rem(x + 2, 4)
    suf = lambda xs, part=pl.ds(4, 4): kvx.at[pl.ds(0, 2), part, xs * 2 + c]
    part_a, part_b = pl.ds(4, 2), pl.ds(6, 2)
    pre_plan = {
        "own_s": (pre(0), pre(0), 0, sibling),
        "own_r": (pre(0), pre(1), 1, right),
        "own_l": (pre(0), pre(2), 2, left),
        "far_r": (raw.at[:, 1, c, low], raw.at[:, 3, c, low], 3, right),
        "far_l": (raw.at[:, 2, c, high], raw.at[:, 3, c, high], 4, left),
        "left_s": (pre(1), pre(1), 5, sibling),
        "right_s": (pre(2), pre(2), 6, sibling),
        "fara_s": (raw.at[:, 3, c, low], raw.at[:, 3, c, low], 7, sibling),
        "farb_s": (raw.at[:, 3, c, high], raw.at[:, 3, c, high], 8, sibling),
    }
    suf_plan = {
        "own_s": (suf(x), suf(x), 0, sibling),
        "own_r": (suf(x), suf(x), 1, right),
        "own_l": (suf(x), suf(x), 2, left),
        "far_r": (suf(xl, part_a), suf(xl, part_a), 3, right),
        "far_l": (suf(xr, part_b), suf(xr, part_b), 4, left),
        "left_s": (suf(xl), suf(xl), 5, sibling),
        "right_s": (suf(xr), suf(xr), 6, sibling),
        "fara_s": (suf(xf, part_a), suf(xf, part_a), 7, sibling),
        "farb_s": (suf(xf, part_b), suf(xf, part_b), 8, sibling),
    }

    def pre_copy(name):
        src, dst, number, device = pre_plan[name]
        return remote(src, dst, pre_send.at[number], pre_recv.at[number], device)

    def suf_copy(name):
        src, dst, number, device = suf_plan[name]
        return remote(src, dst, suf_send.at[number], suf_recv.at[number], device)

    def wait_queries(i, number, half=None):
        part = q_raw.at[i] if half is None else q_raw.at[i, :, half * HALF:(half + 1) * HALF]
        pltpu.make_async_copy(part, part, q_recv.at[number]).wait()
        prepare_queries(i, *((0, GROUP) if half is None else (half * GROUP // 2, (half + 1) * GROUP // 2)))

    own_q.wait()
    prepare_queries(z)
    pl.semaphore_wait(barrier, len(greeted))

    @pl.when(z == 0)
    def _():
        for copy in seen_copies + [own_seen]:
            copy.start()

    for copy in page_copies + q_copies[0::2]:
        copy.start()
    pltpu.make_async_copy(paged, paged, py_recv).wait()
    for copy in slab_copies + own_slab:
        copy.start()
    own_slot = raw.at[:, 0, c]
    pltpu.make_async_copy(own_slot, own_slot, pg_recv).wait()
    for name in ("own_r", "own_l", "own_s"):
        pre_copy(name).start()
    for copy in q_copies[1::2] + fresh_copies:
        copy.start()
    pltpu.make_async_copy(seen_key, seen_key, se_recv).wait()
    pre_copy("own_s").wait_recv()
    prepare_prefix(0)
    up, down = lax.rem(z + 1, 4), lax.rem(z + 3, 4)

    def phase_a(k, carry):
        for half in range(2):
            @pl.when(k == 1 + half)
            def _():
                wait_queries(up, 1 + half, half)
                wait_queries(down, 3 + half, half)

        blocks = []
        for b in range(4):
            i = jnp.where(k == 0, z, up if b < 2 else down)
            r = jnp.where(k == 0, b * BLOCK, (b % 2) * BLOCK + (k - 1) * HALF)
            blocks.append((i, pl.ds(pl.multiple_of(r, BLOCK), BLOCK)))
        attend(None, 0, 1, first=True, blocks=blocks)
        return carry

    lax.fori_loop(0, 3, phase_a, 0)
    pre_copy("own_r").wait_recv()
    pre_copy("far_r").start()
    pre_copy("left_s").start()
    pre_copy("own_l").wait_recv()
    pre_copy("far_l").start()
    pre_copy("right_s").start()
    own_new = kvx.at[pl.ds(0, 2), pl.ds(4, 4), xc]
    pltpu.make_async_copy(own_new, own_new, fr_recv).wait()
    for name in ("own_r", "own_l", "own_s"):
        suf_copy(name).start()
    for copy in [q_far, own_written] + written_copies:
        copy.start()
    pre_copy("left_s").wait_recv()
    prepare_prefix(1)
    pre_copy("right_s").wait_recv()
    prepare_prefix(2)

    def phase_b(k, carry):
        @pl.when(k < 2)
        def _():
            attend(jnp.where(k == 0, up, down), 1, 2)

        @pl.when(k == 0)
        def _():
            pre_copy("far_r").wait_recv()
            pre_copy("fara_s").start()
            pre_copy("far_l").wait_recv()
            pre_copy("farb_s").start()

        @pl.when(k == 1)
        def _():
            suf_copy("own_r").wait_recv()
            suf_copy("far_r").start()
            suf_copy("left_s").start()
            suf_copy("own_l").wait_recv()
            suf_copy("far_l").start()
            suf_copy("right_s").start()

        @pl.when(k == 2)
        def _():
            i = lax.rem(z + 2, 4)
            wait_queries(i, 5)
            attend(i, 0, 3, first=True)
            suf_copy("far_r").wait_recv()
            suf_copy("fara_s").start()
            suf_copy("far_l").wait_recv()
            suf_copy("farb_s").start()

        return carry

    lax.fori_loop(0, 3, phase_b, 0)
    for name in ("fara_s", "farb_s"):
        pre_copy(name).wait_recv()
    prepare_prefix(3)
    for name in ("own_s", "left_s", "right_s", "fara_s", "farb_s"):
        suf_copy(name).wait_recv()

    def out_copy(i):
        return remote(
            o_buf.at[i], attended.at[0, :, lanes(z * ROWS, ROWS)], o_send.at[i], o_recv, (y, i * 8 + xc)
        )

    def own_out():
        return pltpu.make_async_copy(o_buf.at[z], attended.at[0, :, lanes(z * ROWS, ROWS)], o_recv)

    def phase_c(k, carry):
        i = lax.rem(z + jnp.where(k == 0, 2, jnp.where(k == 1, 1, jnp.where(k == 2, 3, 0))), 4)

        @pl.when(i == 0)
        def _():
            attend(i, 3, 2, diagonal=True)

        lax.fori_loop(
            jnp.where(k == 3, 0, 1), jnp.where(i == 3, 2, 1), lambda u, done: (attend(i, 1 + 2 * u, 2), done)[1], 0
        )

        @pl.when(lax.rem(i, 2) == 1)
        def _():
            attend(i, 2 + i, 3, diagonal=True)

        @pl.when(i == 2)
        def _():
            attend(i, 3, 4, diagonal=True)

        for head in range(GROUP):
            rows = slice(head * TOK, (head + 1) * TOK)
            o_buf[i, :, head * HD:(head + 1) * HD] = (
                acc[i, rows, 0:HD] / acc[i, rows, HD:2 * HD]
            ).astype(jnp.bfloat16)

        @pl.when(k < 3)
        def _():
            out_copy(i).start()

        @pl.when(k == 3)
        def _():
            own_out().start()

        return carry

    lax.fori_loop(0, 4, phase_c, 0)

    for copy in page_copies + slab_copies + fresh_copies + q_copies + [q_far] + written_copies:
        copy.wait_send()

    @pl.when(z == 0)
    def _():
        for copy in seen_copies:
            copy.wait_send()

    for name in pre_plan:
        pre_copy(name).wait_send()
        suf_copy(name).wait_send()
    pltpu.make_async_copy(written, written, np_recv).wait()
    for dz in (1, 3, 2):
        out_copy(lax.rem(z + dz, 4)).wait_send()
    pltpu.make_async_copy(attended, attended, o_recv).wait()


def hand_over(attended_in, written_in, attended, written, rows_buf, pages_buf, sems):
    parts = [(attended_in.at[0, part], rows_buf.at[part], attended.at[0, part]) for part in (pl.ds(32 * k, 32) for k in range(4))]
    parts.append((written_in, pages_buf, written))
    arrive = [pltpu.make_async_copy(a, b, sems.at[0, k]) for k, (a, b, _) in enumerate(parts)]
    leave = [pltpu.make_async_copy(b, a, sems.at[1, k]) for k, (_, b, a) in enumerate(parts)]
    for copy in arrive:
        copy.start()
    for one, other in zip(arrive, leave):
        one.wait()
        other.start()
    for copy in leave:
        copy.wait()


def per_device(queries, fresh_cache, page_store, page_table, prefix_lengths):
    anywhere = pl.BlockSpec(memory_space=pl.ANY)
    bf16, f32 = jnp.bfloat16, jnp.float32
    dma = pltpu.SemaphoreType.DMA
    outs_shape = (
        jax.ShapeDtypeStruct((1, TOK, H * HD), bf16),
        jax.ShapeDtypeStruct((1, 4, 1, PAGE, 2 * KVH * HD), bf16),
    )
    outs = pl.pallas_call(
        kernel,
        out_shape=outs_shape,
        in_specs=[
            anywhere, anywhere, anywhere,
            pl.BlockSpec(memory_space=pltpu.VMEM),
            pl.BlockSpec(memory_space=pltpu.SMEM),
        ],
        out_specs=(anywhere, anywhere),
        scratch_shapes=[
            pltpu.VMEM((3, 8, 8, 128, HD), bf16),
            pltpu.VMEM((2, 4, 2, 512, HD), bf16),
            pltpu.VMEM((4, TOK, ROWS), bf16),
            pltpu.VMEM((4, ROWS, 2 * HD), bf16),
            pltpu.VMEM((4, ROWS, 2 * HD), f32),
            pltpu.VMEM((4, ROWS, 128), f32),
            pltpu.VMEM((4, TOK, ROWS), bf16),
            pltpu.VMEM((128, 128), f32),
            pltpu.VMEM((4 * PAGE, 2 * KVH * HD), bf16),
            pltpu.VMEM((16, HD), bf16),
            dma((3,)), dma, dma((3,)), dma, dma((6,)), dma, dma((6,)), dma, dma((5,)), dma((6,)), dma((4,)), dma,
            dma((3,)), dma, dma((9,)), dma((9,)), dma((9,)), dma((9,)),
        ],
        compiler_params=pltpu.CompilerParams(
            collective_id=0, has_side_effects=True, vmem_limit_bytes=56 * 2**20
        ),
        cost_estimate=pl.CostEstimate(flops=2 * 2 * 4096 * 6656 * 128, bytes_accessed=4 * 2**20, transcendentals=4096 * 6656),
    )(queries, fresh_cache, page_store, page_table, prefix_lengths)
    return pl.pallas_call(
        hand_over,
        out_shape=outs_shape,
        in_specs=[anywhere, anywhere],
        out_specs=(anywhere, anywhere),
        scratch_shapes=[
            pltpu.VMEM((TOK, H * HD), bf16), pltpu.VMEM((1, 4, 1, PAGE, 2 * KVH * HD), bf16), dma((2, 5))
        ],
    )(*outs)


def solution(mesh):
    placed = (P("req", "blk", None), P("req", "blk", None), P(("req", "blk"), None, None), P(), P())
    return jax.shard_map(
        per_device,
        mesh=mesh,
        in_specs=placed,
        out_specs=(P("req", "blk", None), P("req", None, "blk", None, None)),
        check_vma=False,
    )
```

```python
import functools
import math

import jax
import jax.numpy as jnp
from jax import lax
from jax.experimental import pallas as pl
from jax.experimental.pallas import tpu as pltpu
from jax.sharding import PartitionSpec as P

H = 32
KVH = 4
HD = 128
GROUP = H // KVH
TOK = 128
PAGE = 32
CHUNK = 1024
ROWS = GROUP * TOK
HALF = ROWS // 2
NEG = -1e30
SCALE = math.log2(math.e) / math.sqrt(HD)
MESH = pl.DeviceIdType.MESH
BLOCK = 256


def kernel(
    queries, fresh, pages, table, lengths, attended, written,
    kvx, raw, q_raw, q_two, acc, top, o_buf, limits,
    paged, seen_key, se_send, se_recv, py_send, py_recv, pg_send, pg_recv, fr_send, fr_recv, q_send, q_recv, o_send, o_recv,
    np_send, np_recv, pre_send, pre_recv, suf_send, suf_recv,
):
    y = lax.axis_index("req")
    blk = lax.axis_index("blk")
    z, x, c = blk // 8, (blk // 2) % 4, blk % 2

    def at(dy, dz, dx, dc):
        z2, x2 = lax.rem(z + dz, 4), lax.rem(x + dx, 4)
        c2 = 1 - c if dc else c
        return (lax.rem(y + dy, 4), z2 * 8 + x2 * 2 + c2)

    def remote(src, dst, send, recv, device):
        return pltpu.make_async_remote_copy(
            src_ref=src, dst_ref=dst, send_sem=send, recv_sem=recv,
            device_id=device, device_id_type=MESH,
        )

    right, left, sibling = at(0, 0, 1, 0), at(0, 0, 3, 0), at(0, 0, 0, 1)
    greeted = [at(dy, 0, 0, 0) for dy in (1, 3, 2)] + [at(0, dz, 0, 0) for dz in (1, 3, 2)]
    greeted += [right, left, sibling]
    barrier = pltpu.get_barrier_semaphore()
    for device in greeted:
        pl.semaphore_signal(barrier, inc=1, device_id=device, device_id_type=MESH)

    def lanes(first, size=HD):
        return pl.ds(pl.multiple_of(first, HD), size)

    def page_rows(first):
        return pl.ds(pl.multiple_of(first * PAGE, PAGE), PAGE)

    xc = x * 2 + c
    slab = pl.ds(pl.multiple_of(z * TOK, TOK), TOK)
    page_copies, slab_copies, fresh_copies, written_copies = [], [], [], []
    for k, dy in enumerate((1, 3, 2)):
        y2 = lax.rem(y + dy, 4)
        page_copies.append(remote(
            pages.at[y2], paged.at[page_rows(y)], py_send.at[k], py_recv, at(dy, 0, 0, 0)
        ))
        written_copies.append(remote(
            fresh.at[0, page_rows(y2)], written.at[0, y, 0], np_send.at[k], np_recv, at(dy, 0, 0, 0)
        ))
    own_page = pltpu.make_async_copy(pages.at[y], paged.at[page_rows(y)], py_recv)
    own_written = pltpu.make_async_copy(fresh.at[0, page_rows(y)], written.at[0, y, 0], np_recv)
    q_copies, seen_copies = [], []
    for k, dz in enumerate((1, 3, 2)):
        z2 = lax.rem(z + dz, 4)
        for plane in range(2):
            head = lanes(plane * 512 + z2 * HD)
            slab_copies.append(remote(
                paged.at[:, head], raw.at[plane, 0, c, slab], pg_send.at[2 * k + plane], pg_recv, at(0, dz, 0, 0)
            ))
            fresh_copies.append(remote(
                fresh.at[0, :, head], kvx.at[plane, 4 + z, xc], fr_send.at[2 * k + plane], fr_recv, at(0, dz, 0, 0)
            ))
        if dz == 2:
            q_far = remote(
                queries.at[0, :, lanes(z2 * ROWS, ROWS)], q_raw.at[z], q_send.at[4], q_recv.at[5], at(0, dz, 0, 0)
            )
        else:
            for half in range(2):
                q_copies.append(remote(
                    queries.at[0, :, lanes(z2 * ROWS + half * HALF, HALF)],
                    q_raw.at[z, :, half * HALF:(half + 1) * HALF],
                    q_send.at[2 * k + half], q_recv.at[{1: 3, 3: 1}[dz] + half], at(0, dz, 0, 0),
                ))
        seen_copies.append(remote(
            fresh.at[0, 0:16, lanes(z2 * HD)], seen_key, se_send.at[k], se_recv, at(0, dz, 0, 0)
        ))
    own_seen = pltpu.make_async_copy(fresh.at[0, 0:16, lanes(z * HD)], seen_key, se_recv)
    own_slab, own_fresh = [], []
    for plane in range(2):
        head = lanes(plane * 512 + z * HD)
        own_slab.append(pltpu.make_async_copy(paged.at[:, head], raw.at[plane, 0, c, slab], pg_recv))
        own_fresh.append(pltpu.make_async_copy(fresh.at[0, :, head], kvx.at[plane, 4 + z, xc], fr_recv))
    own_q = pltpu.make_async_copy(queries.at[0, :, lanes(z * ROWS, ROWS)], q_raw.at[z], q_recv.at[0])
    for copy in [own_q, own_page] + own_fresh:
        copy.start()

    length = lengths[y]
    j = lax.broadcasted_iota(jnp.int32, (128, 128), 0)
    rel = j // 32
    x_of = lax.rem(x + jnp.where(rel == 0, 0, jnp.where(rel == 1, 3, jnp.where(rel == 2, 1, 2))), 4)
    c_of = (j // 16) % 2
    z_of, y_of = (j // 4) % 4, j % 4
    slot = 4 * (y_of * 32 + z_of * 8 + x_of * 2 + c_of) + y
    page = lax.broadcasted_iota(jnp.int32, (128, 128), 1)
    match = jnp.broadcast_to(table[pl.ds(y, 1), :], (128, 128)) == slot
    place = jnp.sum(jnp.where(match, page, 0).astype(jnp.float32), axis=1, keepdims=True)
    limits[...] = jnp.broadcast_to(length.astype(jnp.float32) - PAGE * place, (128, 128))
    ones = jnp.ones((8, 128, 128), jnp.bfloat16)
    for chunk in range(4, 8):
        kvx[2, chunk] = ones

    def prepare_queries(i, first=0, last=GROUP):
        for head in range(first, last):
            block = q_raw[i, :, head * HD:(head + 1) * HD].astype(jnp.float32) * SCALE
            high = block.astype(jnp.bfloat16)
            low = (block - high.astype(jnp.float32)).astype(jnp.bfloat16)
            q_two[i, head * TOK:(head + 1) * TOK, 0:HD] = high
            q_two[i, head * TOK:(head + 1) * TOK, HD:2 * HD] = low

    def prepare_prefix(chunk, first=0, last=8):
        seen = seen_key[...].astype(jnp.float32)[0:1, :]
        row = lax.broadcasted_iota(jnp.int32, (PAGE, 128), 0).astype(jnp.float32)

        def one_block(b, carry):
            for p in range(4):
                limit = limits[pl.ds(chunk * 32 + b * 4 + p, 1), :]
                valid = row < limit
                source = pl.ds(pl.multiple_of(lax.rem(b, 4) * 128 + p * PAGE, PAGE), PAGE)
                key = raw[0, chunk, b // 4, source, :].astype(jnp.float32)
                value = raw[1, chunk, b // 4, source, :].astype(jnp.float32)
                rows = pl.ds(p * PAGE, PAGE)
                kvx[0, chunk, b, rows, :] = jnp.where(valid, key, seen).astype(jnp.bfloat16)
                kvx[1, chunk, b, rows, :] = jnp.where(valid, value, 0.0).astype(jnp.bfloat16)
                kvx[2, chunk, b, rows, :] = jnp.where(valid, 1.0, 0.0).astype(jnp.bfloat16)
            return carry

        lax.fori_loop(first, last, one_block, 0)

    def attend(i, chunk, count, first=False, diagonal=False, blocks=None, half=None):
        blocks = blocks or [(i, slice(r, r + BLOCK)) for r in range(0, ROWS, BLOCK)]
        width = count * (CHUNK if half is None else CHUNK // 2)
        part = pl.ds(0, 8) if half is None else pl.ds(half * 4, 4)

        def scores(i, rows):
            key = kvx[0, pl.ds(chunk, count), part].reshape(width, HD)
            two = jnp.concatenate([key, key], axis=1)
            return lax.dot_general(
                q_two[i, rows, :], two, (((1,), (1,)), ((), ())),
                preferred_element_type=jnp.float32,
            )

        def absorb(i, rows, s):
            if diagonal:
                token = lax.broadcasted_iota(jnp.int32, (BLOCK, CHUNK), 0) % TOK
                key_at = lax.broadcasted_iota(jnp.int32, (BLOCK, CHUNK), 1)
                cut = jnp.where(key_at - token <= xc * TOK, s[:, width - CHUNK:], NEG)
                s = cut if count == 1 else jnp.concatenate([s[:, :width - CHUNK], cut], axis=1)
            value = jnp.concatenate(
                [kvx[plane, pl.ds(chunk, count), part].reshape(width, HD) for plane in (1, 2)], axis=1
            )
            highest = jnp.max(s, axis=1, keepdims=True)
            if not first:
                before = top[i, rows, :][:, :1]
                highest = jnp.maximum(before, highest)
            weights = jnp.exp2(s - highest).astype(jnp.bfloat16)
            top[i, rows, :] = jnp.broadcast_to(highest, (BLOCK, 128))
            added = jnp.dot(weights, value, preferred_element_type=jnp.float32)
            if first:
                acc[i, rows, :] = added
            else:
                acc[i, rows, :] = acc[i, rows, :] * jnp.exp2(before - highest) + added

        waiting = None
        for i, rows in blocks:
            s = scores(i, rows)
            if waiting is not None:
                absorb(*waiting)
            waiting = (i, rows, s)
        absorb(*waiting)

    pre = lambda rel_x: raw.at[:, rel_x, c]
    low, high = pl.ds(0, 256), pl.ds(256, 256)
    xl, xr, xf = lax.rem(x + 3, 4), lax.rem(x + 1, 4), lax.rem(x + 2, 4)
    suf = lambda xs, part=pl.ds(4, 4): kvx.at[pl.ds(0, 2), part, xs * 2 + c]
    part_a, part_b = pl.ds(4, 2), pl.ds(6, 2)
    pre_plan = {
        "own_s": (pre(0), pre(0), 0, sibling),
        "own_r": (pre(0), pre(1), 1, right),
        "own_l": (pre(0), pre(2), 2, left),
        "far_r": (raw.at[:, 1, c, low], raw.at[:, 3, c, low], 3, right),
        "far_l": (raw.at[:, 2, c, high], raw.at[:, 3, c, high], 4, left),
        "left_s": (pre(1), pre(1), 5, sibling),
        "right_s": (pre(2), pre(2), 6, sibling),
        "fara_s": (raw.at[:, 3, c, low], raw.at[:, 3, c, low], 7, sibling),
        "farb_s": (raw.at[:, 3, c, high], raw.at[:, 3, c, high], 8, sibling),
    }
    suf_plan = {
        "own_s": (suf(x), suf(x), 0, sibling),
        "own_r": (suf(x), suf(x), 1, right),
        "own_l": (suf(x), suf(x), 2, left),
        "far_r": (suf(xl, part_a), suf(xl, part_a), 3, right),
        "far_l": (suf(xr, part_b), suf(xr, part_b), 4, left),
        "left_s": (suf(xl), suf(xl), 5, sibling),
        "right_s": (suf(xr), suf(xr), 6, sibling),
        "fara_s": (suf(xf, part_a), suf(xf, part_a), 7, sibling),
        "farb_s": (suf(xf, part_b), suf(xf, part_b), 8, sibling),
    }

    def pre_copy(name):
        src, dst, number, device = pre_plan[name]
        return remote(src, dst, pre_send.at[number], pre_recv.at[number], device)

    def suf_copy(name):
        src, dst, number, device = suf_plan[name]
        return remote(src, dst, suf_send.at[number], suf_recv.at[number], device)

    def wait_queries(i, number, half=None):
        part = q_raw.at[i] if half is None else q_raw.at[i, :, half * HALF:(half + 1) * HALF]
        pltpu.make_async_copy(part, part, q_recv.at[number]).wait()
        prepare_queries(i, *((0, GROUP) if half is None else (half * GROUP // 2, (half + 1) * GROUP // 2)))

    own_q.wait()
    prepare_queries(z)
    pl.semaphore_wait(barrier, len(greeted))

    @pl.when(z == 0)
    def _():
        for copy in seen_copies + [own_seen]:
            copy.start()

    for copy in page_copies + fresh_copies:
        copy.start()
    pltpu.make_async_copy(paged, paged, py_recv).wait()
    for copy in slab_copies + own_slab:
        copy.start()
    own_new = kvx.at[pl.ds(0, 2), pl.ds(4, 4), xc]
    pltpu.make_async_copy(own_new, own_new, fr_recv).wait()
    for name in ("own_r", "own_l", "own_s"):
        suf_copy(name).start()
    own_slot = raw.at[:, 0, c]
    pltpu.make_async_copy(own_slot, own_slot, pg_recv).wait()
    for name in ("own_r", "own_l", "own_s"):
        pre_copy(name).start()
    for copy in q_copies[0::2] + q_copies[1::2]:
        copy.start()
    pltpu.make_async_copy(seen_key, seen_key, se_recv).wait()
    pre_copy("own_s").wait_recv()
    prepare_prefix(0)
    up, down = lax.rem(z + 1, 4), lax.rem(z + 3, 4)

    ring = (("own_r", "far_r", "left_s"), ("own_l", "far_l", "right_s"))

    def phase_a(k, carry):
        for half in range(2):
            @pl.when(k == 1 + half)
            def _():
                wait_queries(up, 1 + half, half)
                wait_queries(down, 3 + half, half)

        @pl.when(k == 2)
        def _():
            for name, far, across in ring:
                suf_copy(name).wait_recv()
                suf_copy(far).start()
                suf_copy(across).start()
            for copy in [q_far, own_written] + written_copies:
                copy.start()

        blocks = []
        for b in range(4):
            i = jnp.where(k == 0, z, up if b < 2 else down)
            r = jnp.where(k == 0, b * BLOCK, (b % 2) * BLOCK + (k - 1) * HALF)
            blocks.append((i, pl.ds(pl.multiple_of(r, BLOCK), BLOCK)))
        attend(None, 0, 1, first=True, blocks=blocks)

        return carry

    lax.fori_loop(0, 3, phase_a, 0)
    for name, far, across in ring:
        pre_copy(name).wait_recv()
        pre_copy(far).start()
        pre_copy(across).start()
    prepare_prefix(1, c * 4, c * 4 + 4)
    prepare_prefix(2, c * 4, c * 4 + 4)

    def phase_b(k, carry):
        @pl.when(k != 1)
        def _():
            attend(up, 1, 2, half=jnp.where(k == 0, c, 1 - c))

        @pl.when(k == 0)
        def _():
            other = 4 - c * 4
            pre_copy("left_s").wait_recv()
            prepare_prefix(1, other, other + 4)
            pre_copy("right_s").wait_recv()
            prepare_prefix(2, other, other + 4)

        @pl.when(k == 1)
        def _():
            attend(down, 1, 2)
            for name, across in (("far_r", "fara_s"), ("far_l", "farb_s")):
                suf_copy(name).wait_recv()
                suf_copy(across).start()

        return carry

    lax.fori_loop(0, 3, phase_b, 0)
    for name, across in (("far_r", "fara_s"), ("far_l", "farb_s")):
        pre_copy(name).wait_recv()
        pre_copy(across).start()
    opposite = lax.rem(z + 2, 4)
    wait_queries(opposite, 5)
    attend(opposite, 0, 3, first=True)
    for name in ("fara_s", "farb_s"):
        pre_copy(name).wait_recv()
    prepare_prefix(3)
    for name in ("own_s", "left_s", "right_s", "fara_s", "farb_s"):
        suf_copy(name).wait_recv()

    def out_copy(i):
        return remote(
            o_buf.at[i], attended.at[0, :, lanes(z * ROWS, ROWS)], o_send.at[i], o_recv, (y, i * 8 + xc)
        )

    def own_out():
        return pltpu.make_async_copy(o_buf.at[z], attended.at[0, :, lanes(z * ROWS, ROWS)], o_recv)

    def phase_c(k, carry):
        i = lax.rem(z + jnp.where(k == 0, 2, jnp.where(k == 1, 1, jnp.where(k == 2, 3, 0))), 4)

        @pl.when(i == 0)
        def _():
            attend(i, 3, 2, diagonal=True)

        lax.fori_loop(
            jnp.where(k == 3, 0, 1), jnp.where(i == 3, 2, 1), lambda u, done: (attend(i, 1 + 2 * u, 2), done)[1], 0
        )

        @pl.when(lax.rem(i, 2) == 1)
        def _():
            attend(i, 2 + i, 3, diagonal=True)

        @pl.when(i == 2)
        def _():
            attend(i, 3, 4, diagonal=True)

        for head in range(GROUP):
            rows = slice(head * TOK, (head + 1) * TOK)
            o_buf[i, :, head * HD:(head + 1) * HD] = (
                acc[i, rows, 0:HD] / acc[i, rows, HD:2 * HD]
            ).astype(jnp.bfloat16)

        @pl.when(k < 3)
        def _():
            out_copy(i).start()

        @pl.when(k == 3)
        def _():
            own_out().start()

        return carry

    lax.fori_loop(0, 4, phase_c, 0)

    for copy in page_copies + slab_copies + fresh_copies + q_copies + [q_far] + written_copies:
        copy.wait_send()

    @pl.when(z == 0)
    def _():
        for copy in seen_copies:
            copy.wait_send()

    for name in pre_plan:
        pre_copy(name).wait_send()
    for name in suf_plan:
        suf_copy(name).wait_send()
    pltpu.make_async_copy(written, written, np_recv).wait()
    for dz in (1, 3, 2):
        out_copy(lax.rem(z + dz, 4)).wait_send()
    pltpu.make_async_copy(attended, attended, o_recv).wait()


def hand_over(attended_in, written_in, attended, written, rows_buf, pages_buf, sems):
    parts = [(attended_in.at[0, part], rows_buf.at[part], attended.at[0, part]) for part in (pl.ds(32 * k, 32) for k in range(4))]
    parts.append((written_in, pages_buf, written))
    arrive = [pltpu.make_async_copy(a, b, sems.at[0, k]) for k, (a, b, _) in enumerate(parts)]
    leave = [pltpu.make_async_copy(b, a, sems.at[1, k]) for k, (_, b, a) in enumerate(parts)]
    for copy in arrive:
        copy.start()
    for one, other in zip(arrive, leave):
        one.wait()
        other.start()
    for copy in leave:
        copy.wait()


def per_device(queries, fresh_cache, page_store, page_table, prefix_lengths):
    anywhere = pl.BlockSpec(memory_space=pl.ANY)
    bf16, f32 = jnp.bfloat16, jnp.float32
    dma = pltpu.SemaphoreType.DMA
    outs_shape = (
        jax.ShapeDtypeStruct((1, TOK, H * HD), bf16),
        jax.ShapeDtypeStruct((1, 4, 1, PAGE, 2 * KVH * HD), bf16),
    )
    outs = pl.pallas_call(
        kernel,
        out_shape=outs_shape,
        in_specs=[
            anywhere, anywhere, anywhere,
            pl.BlockSpec(memory_space=pltpu.VMEM),
            pl.BlockSpec(memory_space=pltpu.SMEM),
        ],
        out_specs=(anywhere, anywhere),
        scratch_shapes=[
            pltpu.VMEM((3, 8, 8, 128, HD), bf16),
            pltpu.VMEM((2, 4, 2, 512, HD), bf16),
            pltpu.VMEM((4, TOK, ROWS), bf16),
            pltpu.VMEM((4, ROWS, 2 * HD), bf16),
            pltpu.VMEM((4, ROWS, 2 * HD), f32),
            pltpu.VMEM((4, ROWS, 128), f32),
            pltpu.VMEM((4, TOK, ROWS), bf16),
            pltpu.VMEM((128, 128), f32),
            pltpu.VMEM((4 * PAGE, 2 * KVH * HD), bf16),
            pltpu.VMEM((16, HD), bf16),
            dma((3,)), dma, dma((3,)), dma, dma((6,)), dma, dma((6,)), dma, dma((5,)), dma((6,)), dma((4,)), dma,
            dma((3,)), dma, dma((9,)), dma((9,)), dma((9,)), dma((9,)),
        ],
        compiler_params=pltpu.CompilerParams(
            collective_id=0, has_side_effects=True, vmem_limit_bytes=56 * 2**20
        ),
        cost_estimate=pl.CostEstimate(flops=2 * 2 * 4096 * 6656 * 128, bytes_accessed=4 * 2**20, transcendentals=4096 * 6656),
    )(queries, fresh_cache, page_store, page_table, prefix_lengths)
    return pl.pallas_call(
        hand_over,
        out_shape=outs_shape,
        in_specs=[anywhere, anywhere],
        out_specs=(anywhere, anywhere),
        scratch_shapes=[
            pltpu.VMEM((TOK, H * HD), bf16), pltpu.VMEM((1, 4, 1, PAGE, 2 * KVH * HD), bf16), dma((2, 5))
        ],
    )(*outs)


def solution(mesh):
    placed = (P("req", "blk", None), P("req", "blk", None), P(("req", "blk"), None, None), P(), P())
    return jax.shard_map(
        per_device,
        mesh=mesh,
        in_specs=placed,
        out_specs=(P("req", "blk", None), P("req", None, "blk", None, None)),
        check_vma=False,
    )
```

```python
import functools
import math

import jax
import jax.numpy as jnp
from jax import lax
from jax.experimental import pallas as pl
from jax.experimental.pallas import tpu as pltpu
from jax.sharding import PartitionSpec as P

H = 32
KVH = 4
HD = 128
GROUP = H // KVH
TOK = 128
PAGE = 32
CHUNK = 1024
ROWS = GROUP * TOK
HALF = ROWS // 2
NEG = -1e30
SCALE = math.log2(math.e) / math.sqrt(HD)
MESH = pl.DeviceIdType.MESH
BLOCK = 256


def kernel(
    queries, fresh, pages, table, lengths, attended, written,
    kvx, raw, q_raw, q_two, acc, top, o_buf, limits,
    paged, seen_key, se_send, se_recv, py_send, py_recv, pg_send, pg_recv, fr_send, fr_recv, q_send, q_recv, o_send, o_recv,
    np_send, np_recv, pre_send, pre_recv, suf_send, suf_recv,
):
    y = lax.axis_index("req")
    blk = lax.axis_index("blk")
    z, x, c = blk // 8, (blk // 2) % 4, blk % 2

    def at(dy, dz, dx, dc):
        z2, x2 = lax.rem(z + dz, 4), lax.rem(x + dx, 4)
        c2 = 1 - c if dc else c
        return (lax.rem(y + dy, 4), z2 * 8 + x2 * 2 + c2)

    def remote(src, dst, send, recv, device):
        return pltpu.make_async_remote_copy(
            src_ref=src, dst_ref=dst, send_sem=send, recv_sem=recv,
            device_id=device, device_id_type=MESH,
        )

    right, left, sibling = at(0, 0, 1, 0), at(0, 0, 3, 0), at(0, 0, 0, 1)
    greeted = [at(dy, 0, 0, 0) for dy in (1, 3, 2)] + [at(0, dz, 0, 0) for dz in (1, 3, 2)]
    greeted += [right, left, sibling]
    barrier = pltpu.get_barrier_semaphore()
    for device in greeted:
        pl.semaphore_signal(barrier, inc=1, device_id=device, device_id_type=MESH)

    def lanes(first, size=HD):
        return pl.ds(pl.multiple_of(first, HD), size)

    def page_rows(first):
        return pl.ds(pl.multiple_of(first * PAGE, PAGE), PAGE)

    xc = x * 2 + c
    slab = pl.ds(pl.multiple_of(z * TOK, TOK), TOK)
    page_copies, slab_copies, fresh_copies, written_copies = [], [], [], []
    for k, dy in enumerate((1, 3, 2)):
        y2 = lax.rem(y + dy, 4)
        page_copies.append(remote(
            pages.at[y2], paged.at[page_rows(y)], py_send.at[k], py_recv, at(dy, 0, 0, 0)
        ))
        written_copies.append(remote(
            fresh.at[0, page_rows(y2)], written.at[0, y, 0], np_send.at[k], np_recv, at(dy, 0, 0, 0)
        ))
    own_page = pltpu.make_async_copy(pages.at[y], paged.at[page_rows(y)], py_recv)
    own_written = pltpu.make_async_copy(fresh.at[0, page_rows(y)], written.at[0, y, 0], np_recv)
    q_copies, seen_copies = [], []
    for k, dz in enumerate((1, 3, 2)):
        z2 = lax.rem(z + dz, 4)
        for plane in range(2):
            head = lanes(plane * 512 + z2 * HD)
            slab_copies.append(remote(
                paged.at[:, head], raw.at[plane, 0, c, slab], pg_send.at[2 * k + plane], pg_recv, at(0, dz, 0, 0)
            ))
            fresh_copies.append(remote(
                fresh.at[0, :, head], kvx.at[plane, 4 + z, xc], fr_send.at[2 * k + plane], fr_recv, at(0, dz, 0, 0)
            ))
        if dz == 2:
            q_far = remote(
                queries.at[0, :, lanes(z2 * ROWS, ROWS)], q_raw.at[z], q_send.at[4], q_recv.at[5], at(0, dz, 0, 0)
            )
        else:
            for half in range(2):
                q_copies.append(remote(
                    queries.at[0, :, lanes(z2 * ROWS + half * HALF, HALF)],
                    q_raw.at[z, :, half * HALF:(half + 1) * HALF],
                    q_send.at[2 * k + half], q_recv.at[{1: 3, 3: 1}[dz] + half], at(0, dz, 0, 0),
                ))
        seen_copies.append(remote(
            fresh.at[0, 0:16, lanes(z2 * HD)], seen_key, se_send.at[k], se_recv, at(0, dz, 0, 0)
        ))
    own_seen = pltpu.make_async_copy(fresh.at[0, 0:16, lanes(z * HD)], seen_key, se_recv)
    own_slab, own_fresh = [], []
    for plane in range(2):
        head = lanes(plane * 512 + z * HD)
        own_slab.append(pltpu.make_async_copy(paged.at[:, head], raw.at[plane, 0, c, slab], pg_recv))
        own_fresh.append(pltpu.make_async_copy(fresh.at[0, :, head], kvx.at[plane, 4 + z, xc], fr_recv))
    own_q = pltpu.make_async_copy(queries.at[0, :, lanes(z * ROWS, ROWS)], q_raw.at[z], q_recv.at[0])
    for copy in [own_q, own_page] + own_fresh:
        copy.start()

    length = lengths[y]
    j = lax.broadcasted_iota(jnp.int32, (128, 128), 0)
    rel = j // 32
    x_of = lax.rem(x + jnp.where(rel == 0, 0, jnp.where(rel == 1, 3, jnp.where(rel == 2, 1, 2))), 4)
    c_of = (j // 16) % 2
    z_of, y_of = (j // 4) % 4, j % 4
    slot = 4 * (y_of * 32 + z_of * 8 + x_of * 2 + c_of) + y
    page = lax.broadcasted_iota(jnp.int32, (128, 128), 1)
    match = jnp.broadcast_to(table[pl.ds(y, 1), :], (128, 128)) == slot
    place = jnp.sum(jnp.where(match, page, 0).astype(jnp.float32), axis=1, keepdims=True)
    limits[...] = jnp.broadcast_to(length.astype(jnp.float32) - PAGE * place, (128, 128))
    ones = jnp.ones((8, 128, 128), jnp.bfloat16)
    for chunk in range(4, 8):
        kvx[2, chunk] = ones

    def prepare_queries(i, first=0, last=GROUP):
        for head in range(first, last):
            block = q_raw[i, :, head * HD:(head + 1) * HD].astype(jnp.float32) * SCALE
            high = block.astype(jnp.bfloat16)
            low = (block - high.astype(jnp.float32)).astype(jnp.bfloat16)
            q_two[i, head * TOK:(head + 1) * TOK, 0:HD] = high
            q_two[i, head * TOK:(head + 1) * TOK, HD:2 * HD] = low

    def prepare_prefix(chunk, first=0, last=8):
        seen = seen_key[...].astype(jnp.float32)[0:1, :]
        row = lax.broadcasted_iota(jnp.int32, (PAGE, 128), 0).astype(jnp.float32)

        def one_block(b, carry):
            for p in range(4):
                limit = limits[pl.ds(chunk * 32 + b * 4 + p, 1), :]
                valid = row < limit
                source = pl.ds(pl.multiple_of(lax.rem(b, 4) * 128 + p * PAGE, PAGE), PAGE)
                key = raw[0, chunk, b // 4, source, :].astype(jnp.float32)
                value = raw[1, chunk, b // 4, source, :].astype(jnp.float32)
                rows = pl.ds(p * PAGE, PAGE)
                kvx[0, chunk, b, rows, :] = jnp.where(valid, key, seen).astype(jnp.bfloat16)
                kvx[1, chunk, b, rows, :] = jnp.where(valid, value, 0.0).astype(jnp.bfloat16)
                kvx[2, chunk, b, rows, :] = jnp.where(valid, 1.0, 0.0).astype(jnp.bfloat16)
            return carry

        lax.fori_loop(first, last, one_block, 0)

    def attend(i, chunk, count, first=False, diagonal=False, blocks=None, half=None, trim=0):
        blocks = blocks or [(i, slice(r, r + BLOCK)) for r in range(0, ROWS, BLOCK)]
        stored = count * (CHUNK if half is None else CHUNK // 2)
        width, last = stored - trim, CHUNK - trim
        part = pl.ds(0, 8) if half is None else pl.ds(half * 4, 4)

        def scores(i, rows):
            key = kvx[0, pl.ds(chunk, count), part].reshape(stored, HD)[:width]
            two = jnp.concatenate([key, key], axis=1)
            return lax.dot_general(
                q_two[i, rows, :], two, (((1,), (1,)), ((), ())),
                preferred_element_type=jnp.float32,
            )

        def absorb(i, rows, s):
            if diagonal:
                token = lax.broadcasted_iota(jnp.int32, (BLOCK, last), 0) % TOK
                key_at = lax.broadcasted_iota(jnp.int32, (BLOCK, last), 1)
                cut = jnp.where(key_at - token <= xc * TOK, s[:, width - last:], NEG)
                s = cut if count == 1 else jnp.concatenate([s[:, :width - last], cut], axis=1)
            value = jnp.concatenate(
                [kvx[plane, pl.ds(chunk, count), part].reshape(stored, HD)[:width] for plane in (1, 2)], axis=1
            )
            highest = jnp.max(s, axis=1, keepdims=True)
            if not first:
                before = top[i, rows, :][:, :1]
                highest = jnp.maximum(before, highest)
            weights = jnp.exp2(s - highest).astype(jnp.bfloat16)
            top[i, rows, :] = jnp.broadcast_to(highest, (BLOCK, 128))
            added = jnp.dot(weights, value, preferred_element_type=jnp.float32)
            if first:
                acc[i, rows, :] = added
            else:
                acc[i, rows, :] = acc[i, rows, :] * jnp.exp2(before - highest) + added

        waiting = None
        for i, rows in blocks:
            s = scores(i, rows)
            if waiting is not None:
                absorb(*waiting)
            waiting = (i, rows, s)
        absorb(*waiting)

    pre = lambda rel_x: raw.at[:, rel_x, c]
    low, high = pl.ds(0, 256), pl.ds(256, 256)
    xl, xr, xf = lax.rem(x + 3, 4), lax.rem(x + 1, 4), lax.rem(x + 2, 4)
    suf = lambda xs, part=pl.ds(4, 4): kvx.at[pl.ds(0, 2), part, xs * 2 + c]
    part_a, part_b = pl.ds(4, 2), pl.ds(6, 2)
    pre_plan = {
        "own_s": (pre(0), pre(0), 0, sibling),
        "own_r": (pre(0), pre(1), 1, right),
        "own_l": (pre(0), pre(2), 2, left),
        "far_r": (raw.at[:, 1, c, low], raw.at[:, 3, c, low], 3, right),
        "far_l": (raw.at[:, 2, c, high], raw.at[:, 3, c, high], 4, left),
        "left_s": (pre(1), pre(1), 5, sibling),
        "right_s": (pre(2), pre(2), 6, sibling),
        "fara_s": (raw.at[:, 3, c, low], raw.at[:, 3, c, low], 7, sibling),
        "farb_s": (raw.at[:, 3, c, high], raw.at[:, 3, c, high], 8, sibling),
    }
    suf_plan = {
        "own_s": (suf(x), suf(x), 0, sibling),
        "own_r": (suf(x), suf(x), 1, right),
        "own_l": (suf(x), suf(x), 2, left),
        "far_r": (suf(xl, part_a), suf(xl, part_a), 3, right),
        "far_l": (suf(xr, part_b), suf(xr, part_b), 4, left),
        "left_s": (suf(xl), suf(xl), 5, sibling),
        "right_s": (suf(xr), suf(xr), 6, sibling),
        "fara_s": (suf(xf, part_a), suf(xf, part_a), 7, sibling),
        "farb_s": (suf(xf, part_b), suf(xf, part_b), 8, sibling),
    }

    def pre_copy(name):
        src, dst, number, device = pre_plan[name]
        return remote(src, dst, pre_send.at[number], pre_recv.at[number], device)

    def suf_copy(name):
        src, dst, number, device = suf_plan[name]
        return remote(src, dst, suf_send.at[number], suf_recv.at[number], device)

    def wait_queries(i, number, half=None):
        part = q_raw.at[i] if half is None else q_raw.at[i, :, half * HALF:(half + 1) * HALF]
        pltpu.make_async_copy(part, part, q_recv.at[number]).wait()
        prepare_queries(i, *((0, GROUP) if half is None else (half * GROUP // 2, (half + 1) * GROUP // 2)))

    own_q.wait()
    prepare_queries(z)
    pl.semaphore_wait(barrier, len(greeted))

    @pl.when(z == 0)
    def _():
        for copy in seen_copies + [own_seen]:
            copy.start()

    for copy in page_copies + fresh_copies:
        copy.start()
    pltpu.make_async_copy(paged, paged, py_recv).wait()
    for copy in slab_copies + own_slab:
        copy.start()
    own_new = kvx.at[pl.ds(0, 2), pl.ds(4, 4), xc]
    pltpu.make_async_copy(own_new, own_new, fr_recv).wait()
    for name in ("own_r", "own_l", "own_s"):
        suf_copy(name).start()
    own_slot = raw.at[:, 0, c]
    pltpu.make_async_copy(own_slot, own_slot, pg_recv).wait()
    for name in ("own_r", "own_l", "own_s"):
        pre_copy(name).start()
    for copy in q_copies[0::2] + q_copies[1::2]:
        copy.start()
    pltpu.make_async_copy(seen_key, seen_key, se_recv).wait()
    pre_copy("own_s").wait_recv()
    prepare_prefix(0)
    up, down = lax.rem(z + 1, 4), lax.rem(z + 3, 4)

    ring = (("own_r", "far_r", "left_s"), ("own_l", "far_l", "right_s"))

    def phase_a(k, carry):
        for half in range(2):
            @pl.when(k == 1 + half)
            def _():
                wait_queries(up, 1 + half, half)
                wait_queries(down, 3 + half, half)

        @pl.when(k == 2)
        def _():
            for name, far, across in ring:
                suf_copy(name).wait_recv()
                suf_copy(far).start()
                suf_copy(across).start()
            for copy in [q_far, own_written] + written_copies:
                copy.start()

        blocks = []
        for b in range(4):
            i = jnp.where(k == 0, z, up if b < 2 else down)
            r = jnp.where(k == 0, b * BLOCK, (b % 2) * BLOCK + (k - 1) * HALF)
            blocks.append((i, pl.ds(pl.multiple_of(r, BLOCK), BLOCK)))
        attend(None, 0, 1, first=True, blocks=blocks)

        return carry

    lax.fori_loop(0, 3, phase_a, 0)
    for name, far, across in ring:
        pre_copy(name).wait_recv()
        pre_copy(far).start()
        pre_copy(across).start()
    prepare_prefix(1, c * 4, c * 4 + 4)
    prepare_prefix(2, c * 4, c * 4 + 4)

    def phase_b(k, carry):
        @pl.when(k != 1)
        def _():
            attend(up, 1, 2, half=jnp.where(k == 0, c, 1 - c))

        @pl.when(k == 0)
        def _():
            other = 4 - c * 4
            pre_copy("left_s").wait_recv()
            prepare_prefix(1, other, other + 4)
            pre_copy("right_s").wait_recv()
            prepare_prefix(2, other, other + 4)

        @pl.when(k == 1)
        def _():
            attend(down, 1, 2)
            for name, across in (("far_r", "fara_s"), ("far_l", "farb_s")):
                suf_copy(name).wait_recv()
                suf_copy(across).start()

        return carry

    lax.fori_loop(0, 3, phase_b, 0)
    for name, across in (("far_r", "fara_s"), ("far_l", "farb_s")):
        pre_copy(name).wait_recv()
        pre_copy(across).start()
    opposite = lax.rem(z + 2, 4)
    wait_queries(opposite, 5)
    attend(opposite, 0, 3, first=True)
    for name in ("fara_s", "farb_s"):
        pre_copy(name).wait_recv()
    prepare_prefix(3)
    for name in ("own_s", "left_s", "right_s", "fara_s", "farb_s"):
        suf_copy(name).wait_recv()

    def out_copy(i):
        return remote(
            o_buf.at[i], attended.at[0, :, lanes(z * ROWS, ROWS)], o_send.at[i], o_recv, (y, i * 8 + xc)
        )

    def own_out():
        return pltpu.make_async_copy(o_buf.at[z], attended.at[0, :, lanes(z * ROWS, ROWS)], o_recv)

    def phase_c(k, carry):
        i = lax.rem(z + jnp.where(k == 0, 2, jnp.where(k == 1, 1, jnp.where(k == 2, 3, 0))), 4)

        lax.fori_loop(
            jnp.where(k == 3, 0, 1), jnp.where(i == 3, 2, 1), lambda u, done: (attend(i, 1 + 2 * u, 2), done)[1], 0
        )

        for near, trim in ((x < 2, CHUNK // 2), (x >= 2, 0)):
            @pl.when((i == 0) & near)
            def _():
                attend(i, 3, 2, diagonal=True, trim=trim)

            @pl.when((lax.rem(i, 2) == 1) & near)
            def _():
                attend(i, 2 + i, 3, diagonal=True, trim=trim)

            @pl.when((i == 2) & near)
            def _():
                attend(i, 3, 4, diagonal=True, trim=trim)

        for head in range(GROUP):
            rows = slice(head * TOK, (head + 1) * TOK)
            o_buf[i, :, head * HD:(head + 1) * HD] = (
                acc[i, rows, 0:HD] / acc[i, rows, HD:2 * HD]
            ).astype(jnp.bfloat16)

        @pl.when(k < 3)
        def _():
            out_copy(i).start()

        @pl.when(k == 3)
        def _():
            own_out().start()

        return carry

    lax.fori_loop(0, 4, phase_c, 0)

    for copy in page_copies + slab_copies + fresh_copies + q_copies + [q_far] + written_copies:
        copy.wait_send()

    @pl.when(z == 0)
    def _():
        for copy in seen_copies:
            copy.wait_send()

    for name in pre_plan:
        pre_copy(name).wait_send()
    for name in suf_plan:
        suf_copy(name).wait_send()
    pltpu.make_async_copy(written, written, np_recv).wait()
    for dz in (1, 3, 2):
        out_copy(lax.rem(z + dz, 4)).wait_send()
    pltpu.make_async_copy(attended, attended, o_recv).wait()


def hand_over(attended_in, written_in, attended, written, rows_buf, pages_buf, sems):
    parts = [(attended_in.at[0, part], rows_buf.at[part], attended.at[0, part]) for part in (pl.ds(32 * k, 32) for k in range(4))]
    parts.append((written_in, pages_buf, written))
    arrive = [pltpu.make_async_copy(a, b, sems.at[0, k]) for k, (a, b, _) in enumerate(parts)]
    leave = [pltpu.make_async_copy(b, a, sems.at[1, k]) for k, (_, b, a) in enumerate(parts)]
    for copy in arrive:
        copy.start()
    for one, other in zip(arrive, leave):
        one.wait()
        other.start()
    for copy in leave:
        copy.wait()


def per_device(queries, fresh_cache, page_store, page_table, prefix_lengths):
    anywhere = pl.BlockSpec(memory_space=pl.ANY)
    bf16, f32 = jnp.bfloat16, jnp.float32
    dma = pltpu.SemaphoreType.DMA
    outs_shape = (
        jax.ShapeDtypeStruct((1, TOK, H * HD), bf16),
        jax.ShapeDtypeStruct((1, 4, 1, PAGE, 2 * KVH * HD), bf16),
    )
    outs = pl.pallas_call(
        kernel,
        out_shape=outs_shape,
        in_specs=[
            anywhere, anywhere, anywhere,
            pl.BlockSpec(memory_space=pltpu.VMEM),
            pl.BlockSpec(memory_space=pltpu.SMEM),
        ],
        out_specs=(anywhere, anywhere),
        scratch_shapes=[
            pltpu.VMEM((3, 8, 8, 128, HD), bf16),
            pltpu.VMEM((2, 4, 2, 512, HD), bf16),
            pltpu.VMEM((4, TOK, ROWS), bf16),
            pltpu.VMEM((4, ROWS, 2 * HD), bf16),
            pltpu.VMEM((4, ROWS, 2 * HD), f32),
            pltpu.VMEM((4, ROWS, 128), f32),
            pltpu.VMEM((4, TOK, ROWS), bf16),
            pltpu.VMEM((128, 128), f32),
            pltpu.VMEM((4 * PAGE, 2 * KVH * HD), bf16),
            pltpu.VMEM((16, HD), bf16),
            dma((3,)), dma, dma((3,)), dma, dma((6,)), dma, dma((6,)), dma, dma((5,)), dma((6,)), dma((4,)), dma,
            dma((3,)), dma, dma((9,)), dma((9,)), dma((9,)), dma((9,)),
        ],
        compiler_params=pltpu.CompilerParams(
            collective_id=0, has_side_effects=True, vmem_limit_bytes=56 * 2**20
        ),
        cost_estimate=pl.CostEstimate(flops=2 * 2 * 4096 * 6656 * 128, bytes_accessed=4 * 2**20, transcendentals=4096 * 6656),
    )(queries, fresh_cache, page_store, page_table, prefix_lengths)
    return pl.pallas_call(
        hand_over,
        out_shape=outs_shape,
        in_specs=[anywhere, anywhere],
        out_specs=(anywhere, anywhere),
        scratch_shapes=[
            pltpu.VMEM((TOK, H * HD), bf16), pltpu.VMEM((1, 4, 1, PAGE, 2 * KVH * HD), bf16), dma((2, 5))
        ],
    )(*outs)


def solution(mesh):
    placed = (P("req", "blk", None), P("req", "blk", None), P(("req", "blk"), None, None), P(), P())
    return jax.shard_map(
        per_device,
        mesh=mesh,
        in_specs=placed,
        out_specs=(P("req", "blk", None), P("req", None, "blk", None, None)),
        check_vma=False,
    )
```
